128 devices in a mesh: loader: 4 (over y), enc: 32 (over x, z, core).
Axes of the slice: x: 4, y: 4, z: 4, core: 2. Of those that a mesh axis runs over, the one named last changes fastest.
Arguments:
- frames: bfloat16 [256, 128, 64, 128], P('loader', 'enc'), may hold values from -37 to 37
- clip_of_frame: int32 [256], P(('loader', 'enc')), may hold values from 0 to 7, never falling along the last dimension, each value on 1 to 128 neighbouring positions
- norm_gain: float32 [128], replicated, may hold values from 0.1 to 1.9
- norm_bias: float32 [128], replicated, may hold values from -3 to 3
- conv_weight: bfloat16 [3, 3, 3, 128, 128], replicated, may hold values from -0.109375 to 0.109375
- conv_bias: float32 [128], replicated, may hold values from -3 to 3
Outputs:
- latents: bfloat16 [256, 64, 32, 128], P('loader', 'enc')
The draws below stay inside these ranges and needn't reach their ends.
Inputs may be any that keep to these rules, and one draw needn't show every extreme that they name: `clip_of_frame`: clip numbers never fall along the timeline; each clip has 1 to 128 frames, one exactly 128.
All inputs are finite; a program needn't handle non-finite values.
Results may differ from the reference program's by a relative error of at most 0.0013.
The reference program's roundings to bfloat16 on the way (of `act`) count: a program that leaves them out, or rounds other values in their place, can miss the bound.
Values may be sent and summed in bfloat16 or wider, within the bound.
A program may use at most 128 MiB of HBM per device.

```python
import math
import jax
import jax.numpy as jnp
import numpy as np
from jax import lax

C = 128
GROUPS = 32
W = 64
NT = 256
H = 128
CLIPS = 8
CLIP_MOST = 128


def draw_frames(key, part):
    key = jax.random.fold_in(key, 11)
    first_key, second_key, third_key = jax.random.split(key, 3)
    shape = (NT, H, W, C)
    base = jnp.clip(jax.random.normal(first_key, shape, jnp.float32), -4.0, 4.0)
    frame_scale = jnp.exp(jax.random.uniform(second_key, (NT, 1, 1, 1), jnp.float32, math.log(0.3), math.log(3.0)))
    channel_scale = jnp.exp(jax.random.uniform(third_key, (1, 1, 1, C), jnp.float32, math.log(0.3), math.log(3.0)))
    return (base * frame_scale * channel_scale).astype(jnp.bfloat16)


def split_up(amount, total, most, skew):
    portions = [(1 << 20) // math.isqrt(rank ** skew) + 1 for rank in range(2, amount + 1)]
    rest, given = total - most - (amount - 1), [1] * (amount - 1)
    while rest > 0:
        movable = [i for i in range(amount - 1) if given[i] < most]
        pool, remaining = sum([portions[i] for i in movable]), rest
        for i in movable:
            extra = min(most - given[i], max(1, remaining * portions[i] // pool), rest)
            given[i] = given[i] + extra
            rest = rest - extra
    return np.array([most] + given)


def ragged_sizes(rng, count, total, most, slope):
    if count == 2:
        one = jax.random.randint(rng, (), max(1, total - most), min(most, total - 1) + 1)
        return jnp.stack([one, total - one])
    lengths = jnp.asarray(split_up(count, total, most, slope), jnp.int32)
    couples = (count - 1) // 2
    donor, sink = lengths[1:1 + 2 * couples:2], lengths[2:2 + 2 * couples:2]
    room = jnp.minimum(donor - 1, most - sink)
    passed = jax.random.randint(jax.random.fold_in(rng, 1), (couples,), 0, 1 << 20) % (room + 1)
    lengths = lengths.at[1:1 + 2 * couples:2].set(donor - passed).at[2:2 + 2 * couples:2].set(sink + passed)
    return lengths[jax.random.permutation(jax.random.fold_in(rng, 2), count)]


def gaussian(stream_key, extent, deviation, bound, held_as=jnp.bfloat16):
    values = deviation * jax.random.normal(stream_key, extent, jnp.float32)
    return jnp.clip(values, min=-bound, max=bound).astype(held_as)


def setup_inputs(seed: int = 0) -> dict:
    keys = jax.random.split(jax.random.key(seed), 7)
    frames = draw_frames(jax.random.fold_in(keys[6], 71), 0)
    clip_of_frame = jnp.searchsorted(jnp.cumsum(ragged_sizes(keys[1], CLIPS, NT, CLIP_MOST, 0)), jnp.arange(NT), side="right").astype(jnp.int32)
    norm_gain = jnp.clip(1.0 + 0.18 * jax.random.normal(keys[2], (C,), jnp.float32), 0.1, 1.9)
    norm_bias = gaussian(keys[3], (C,), 0.5, 3.0, jnp.float32)
    conv_weight = gaussian(keys[4], (3, 3, 3, C, C), (27 * C) ** -0.5, 0.109375)
    conv_bias = gaussian(keys[5], (C,), 0.5, 3.0, jnp.float32)
    return dict(frames=frames, clip_of_frame=clip_of_frame, norm_gain=norm_gain, norm_bias=norm_bias, conv_weight=conv_weight, conv_bias=conv_bias)


EPS = 1e-06
BLOCK = 8

def conv_block(ext, ids_ext, conv_weight, conv_bias):
    tlen = ext.shape[0] - 2
    out_rows = (ext.shape[1] - 1) // 2
    out_cols = ext.shape[2] // 2
    chans = ext.shape[3]
    padded = jnp.pad(ext, ((0, 0), (0, 0), (1, 0), (0, 0)))
    stacked = jnp.concatenate([padded[:, :, k:k + 2 * out_cols - 1:2, :] for k in range(3)], axis=-1).astype(jnp.float32)
    taps = conv_weight.reshape(3, 3, 3 * chans, chans).astype(jnp.float32)
    total = jnp.zeros((tlen, out_rows, out_cols, chans), jnp.float32)
    for kt in range(3):
        keep = (ids_ext[kt:kt + tlen] == ids_ext[2:]).astype(jnp.float32)
        partial_sum = jnp.zeros((tlen, out_rows, out_cols, chans), jnp.float32)
        for kh in range(3):
            piece = stacked[kt:kt + tlen, kh:kh + 2 * out_rows - 1:2]
            partial_sum = partial_sum + jnp.einsum('thwk,kc->thwc', piece, taps[kt, kh], precision=lax.Precision.HIGHEST)
        total = total + keep[:, None, None, None] * partial_sum
    return (total + conv_bias).astype(jnp.bfloat16)

def reference(frames, clip_of_frame, norm_gain, norm_bias, conv_weight, conv_bias):
    frame_count, rows_all, cols_all, chans = frames.shape
    per_group = chans // GROUPS
    blocked = frames.reshape(frame_count // BLOCK, BLOCK, rows_all, cols_all, chans)

    def frame_sums(block):
        values = block.astype(jnp.float32)
        first = lax.optimization_barrier(jnp.sum(values, axis=(1, 2))).reshape(BLOCK, GROUPS, per_group).sum(-1)
        second = lax.optimization_barrier(jnp.sum(values * values, axis=(1, 2))).reshape(BLOCK, GROUPS, per_group).sum(-1)
        return (first, second)
    first, second = lax.map(frame_sums, blocked)
    first = first.reshape(frame_count, GROUPS)
    second = second.reshape(frame_count, GROUPS)

    def running(carry, item):
        prev_id, acc_first, acc_second, acc_count = carry
        ident, one, two = item
        same = ident == prev_id
        acc_first = jnp.where(same, acc_first + one, one)
        acc_second = jnp.where(same, acc_second + two, two)
        acc_count = jnp.where(same, acc_count + 1.0, jnp.float32(1.0))
        return ((ident, acc_first, acc_second, acc_count), (acc_first, acc_second, acc_count))
    start = (jnp.int32(-1), jnp.zeros((GROUPS,), jnp.float32), jnp.zeros((GROUPS,), jnp.float32), jnp.float32(0.0))
    _, (run_first, run_second, run_count) = lax.scan(running, start, (clip_of_frame, first, second))
    cells = rows_all * cols_all * per_group

    def normalize_block(item):
        block, one, two, count = item
        per = count * cells
        mean = one / per[:, None]
        var = two / per[:, None] - mean * mean
        inverse = lax.rsqrt(var + EPS)
        mean_c = jnp.repeat(mean, per_group, axis=1)
        inverse_c = jnp.repeat(inverse, per_group, axis=1)
        scaled = (block.astype(jnp.float32) - mean_c[:, None, None, :]) * (inverse_c[:, None, None, :] * norm_gain) + norm_bias
        return jax.nn.silu(scaled).astype(jnp.bfloat16)
    act = lax.map(normalize_block, (blocked, run_first.reshape(-1, BLOCK, GROUPS), run_second.reshape(-1, BLOCK, GROUPS), run_count.reshape(-1, BLOCK)))
    act = act.reshape(frame_count, rows_all, cols_all, chans)
    ext = jnp.pad(act, ((2, 0), (1, 0), (0, 0), (0, 0)))
    ids_ext = jnp.concatenate([jnp.full((2,), -1.0, jnp.float32), clip_of_frame.astype(jnp.float32)])

    def encode_block(index):
        begin = (index * BLOCK).astype(jnp.int32)
        piece = lax.dynamic_slice_in_dim(ext, begin, BLOCK + 2, 0)
        ids_piece = lax.dynamic_slice_in_dim(ids_ext, begin, BLOCK + 2, 0)
        return conv_block(piece, ids_piece, conv_weight, conv_bias)
    out = lax.map(encode_block, jnp.arange(frame_count // BLOCK, dtype=jnp.int32))
    return out.reshape(frame_count, rows_all // 2, cols_all // 2, chans)
```

```python
import functools

import jax
import jax.numpy as jnp
from jax import lax
from jax.experimental import pallas as pl
from jax.experimental.pallas import tpu as pltpu
from jax.sharding import PartitionSpec as P

MESH = pl.DeviceIdType.MESH
EPS = 1e-06
GROUP = 4
LOADERS, NX, NK = 4, 4, 8
CHUNK = 8


def spread(values, lane, at):
    only = jnp.where(lane % GROUP == at, values, 0.0)
    width = values.shape[1]
    total = only
    for other in range(GROUP):
        if other != at:
            total = total + pltpu.roll(only, (other - at) % width, axis=1)
    return total


def kernel(
    frames, clips, gain, bias, weight, conv_bias, out,
    x, act, tmp, w, part, gath1, sum1, gath2, sum2, table, scale, shift, keep1, keep2, obuf,
    ids_s, gain_v, bias_v, cbias_v,
    load_sem, small_sem, w_sem, out_sem, send_sem, recv1, recv2, recv3, recvh,
):
    frames_n, rows, cols, chans = frames.shape
    chunks = frames_n // CHUNK
    half = cols // 2
    l, e = lax.axis_index("loader"), lax.axis_index("enc")
    xi, k = e // NK, e % NK
    encs = NX * NK
    l_next, l_prev = (l + 1) % LOADERS, (l + LOADERS - 1) % LOADERS
    e_next, e_prev = (e + 1) % encs, (e + encs - 1) % encs

    loads = []
    for i in range(chunks):
        loads.append(
            pltpu.make_async_copy(
                frames.at[pl.ds(i * CHUNK, CHUNK)],
                x.at[pl.ds(2 + i * CHUNK, CHUNK), pl.ds(1, rows)],
                load_sem.at[i],
            )
        )
        loads[-1].start()
    smalls = [
        pltpu.make_async_copy(clips, ids_s, small_sem.at[0]),
        pltpu.make_async_copy(gain, gain_v, small_sem.at[1]),
        pltpu.make_async_copy(bias, bias_v, small_sem.at[2]),
        pltpu.make_async_copy(conv_bias, cbias_v, small_sem.at[3]),
    ]
    for copy in smalls:
        copy.start()

    barrier = pltpu.get_barrier_semaphore()

    def tell(device):
        pl.semaphore_signal(barrier, inc=1, device_id=device, device_id_type=MESH)

    partners8 = [(l, NK * xi + (k + i) % NK) for i in range(1, NK)]
    partners16 = [
        ((l + a) % LOADERS, NK * ((xi + b) % NX) + k)
        for a in range(LOADERS)
        for b in range(NX)
        if (a, b) != (0, 0)
    ]
    for device in partners8 + partners16 + [(l, e_prev), (l_prev, e_prev)]:
        tell(device)

    weights = [
        pltpu.make_async_copy(weight.at[:, :, 1], w.at[:, :, pl.ds(0, chans), pl.ds(0, chans)], w_sem.at[0]),
        pltpu.make_async_copy(weight.at[:, :, 2], w.at[:, :, pl.ds(chans, chans), pl.ds(0, chans)], w_sem.at[1]),
        pltpu.make_async_copy(weight.at[:, :, 0], w.at[:, :, pl.ds(chans, chans), pl.ds(chans, chans)], w_sem.at[2]),
    ]
    for copy in weights:
        copy.start()
    w[:, :, :chans, chans:] = jnp.zeros((3, 3, chans, chans), jnp.bfloat16)

    lane8 = lax.broadcasted_iota(jnp.int32, (CHUNK, chans), 1)
    row8 = lax.broadcasted_iota(jnp.int32, (CHUNK, chans), 0)
    smalls[0].wait()
    id_a, id_b = ids_s[0].astype(jnp.float32), ids_s[1].astype(jnp.float32)
    for i in range(chunks):
        loads[i].wait()
        values = x[pl.ds(2 + i * CHUNK, CHUNK), pl.ds(1, rows)].astype(jnp.float32)
        first = jnp.sum(values, axis=(1, 2))
        second = jnp.sum(values * values, axis=(1, 2))
        for by in (1, 2):
            first = first + pltpu.roll(first, chans - by, axis=1)
            second = second + pltpu.roll(second, chans - by, axis=1)
        second = pltpu.roll(second, 1, axis=1)
        ident = jnp.where(
            row8 + i * CHUNK == 2 * e, id_a, jnp.where(row8 + i * CHUNK == 2 * e + 1, id_b, 0.0)
        )
        role = lane8 % GROUP
        part[i] = jnp.where(
            role == 0, first, jnp.where(role == 1, second, jnp.where(role == 2, ident, 0.0))
        )

    pl.semaphore_wait(barrier, 24)

    def send(src, dst, at, recv, device):
        copy = pltpu.make_async_remote_copy(
            src_ref=src, dst_ref=dst, send_sem=send_sem.at[at], recv_sem=recv,
            device_id=device, device_id_type=MESH,
        )
        copy.start()
        return copy

    sent = []
    for i, device in enumerate(partners8):
        sent.append(
            send(part.at[(k + i + 1) % NK], gath1.at[k], i, recv1.at[k], device)
        )
    sent.append(
        send(frames.at[:, rows - 1], x.at[pl.ds(2, frames_n), 0], 29, recvh.at[0], (l, e_next))
    )
    sent.append(
        send(frames.at[pl.ds(frames_n - 2, 2)], x.at[pl.ds(0, 2), pl.ds(1, rows)], 30, recvh.at[1], (l_next, e))
    )
    sent.append(
        send(frames.at[pl.ds(frames_n - 2, 2), rows - 1], x.at[pl.ds(0, 2), 0], 31, recvh.at[2], (l_next, e_next))
    )

    def arrived(ref, sem):
        pltpu.make_async_copy(ref, ref, sem).wait()

    gath1[k] = part[k]
    for i in range(1, NK):
        slot = (k + i) % NK
        arrived(gath1.at[slot], recv1.at[slot])
    sum1[...] = jnp.sum(gath1[...], axis=0)

    mine = l * NX + xi
    for i, device in enumerate(partners16):
        sent.append(send(sum1, gath2.at[mine], 7 + i, recv2.at[mine], device))
    gath2[mine] = sum1[...]
    for a in range(LOADERS):
        for b in range(NX):
            if (a, b) != (0, 0):
                slot = ((l + a) % LOADERS) * NX + (xi + b) % NX
                arrived(gath2.at[slot], recv2.at[slot])
    for a in range(LOADERS):
        sum2[a] = gath2[a * NX] + gath2[a * NX + 1] + gath2[a * NX + 2] + gath2[a * NX + 3]

    for i, device in enumerate(partners8):
        sent.append(send(sum2, table.at[pl.ds(1, LOADERS), k], 22 + i, recv3.at[k], device))
    for a in range(LOADERS):
        table[1 + a, k] = sum2[a]
    table[0, NK - 1] = jnp.full((CHUNK, chans), -1.0, jnp.float32)
    for copy in smalls[1:]:
        copy.wait()
    for i in range(1, NK):
        slot = (k + i) % NK
        arrived(sum2, recv3.at[slot])

    total = LOADERS * frames_n
    lane_all = lax.broadcasted_iota(jnp.int32, (total, chans), 1) % GROUP
    everything = table[pl.ds(1, LOADERS)].reshape(total, chans)
    everything = jnp.where(lane_all == 3, 1.0, everything)
    count = frames_n + CHUNK
    here = jnp.concatenate([table[l, NK - 1], table[l + 1].reshape(frames_n, chans)], axis=0)
    lane = lax.broadcasted_iota(jnp.int32, (count, chans), 1)
    ids_col = spread(here, lane, 2)
    picks = jnp.where(lane == 2, 1.0, 0.0).astype(jnp.bfloat16)
    ids_row = lax.dot_general(
        picks, everything.astype(jnp.bfloat16), (((1,), (1,)), ((), ())), preferred_element_type=jnp.float32
    )
    at_col = lax.broadcasted_iota(jnp.int32, (count, total), 1)
    at_row = lax.broadcasted_iota(jnp.int32, (count, total), 0) + (l * frames_n - CHUNK)
    same = ids_row == jnp.concatenate([ids_col] * (total // chans), axis=1)
    member = jnp.where(same & (at_col <= at_row), 1.0, 0.0)
    run = jnp.dot(member, everything, precision=lax.Precision.HIGHEST, preferred_element_type=jnp.float32)
    per = jnp.maximum(spread(run, lane, 3), 1.0) * float(encs * rows * cols * GROUP)
    mean = spread(run, lane, 0) / per
    var = spread(run, lane, 1) / per - mean * mean
    times = lax.rsqrt(var + EPS) * gain_v[...]
    scale[...] = 0.5 * times
    shift[...] = 0.5 * (bias_v[...] - mean * times)
    tmp[0, pl.ds(0, count)] = ids_col
    own = tmp[0, pl.ds(CHUNK, frames_n)]
    keep1[...] = jnp.where(tmp[0, pl.ds(CHUNK - 1, frames_n)] == own, 1.0, 0.0)
    keep2[...] = jnp.where(tmp[0, pl.ds(CHUNK - 2, frames_n)] == own, 1.0, 0.0)

    def activate(frame, row, slot, live=None):
        h = x[frame, row].astype(jnp.float32) * scale[pl.ds(frame + CHUNK - 2, 1)] + shift[pl.ds(frame + CHUNK - 2, 1)]
        v = h + h * jnp.tanh(h)
        if live is not None:
            v = jnp.where(live, v, 0.0)
        tmp[slot, pl.ds(0, cols)] = v
        act[frame, row, :, pl.ds(0, chans)] = tmp[slot, pl.ds(0, half, stride=2)].astype(jnp.bfloat16)
        act[frame, row, :, pl.ds(chans, chans)] = tmp[slot, pl.ds(1, half, stride=2)].astype(jnp.bfloat16)

    positions = CHUNK * half
    inner = lax.broadcasted_iota(jnp.int32, (positions, chans), 0) % half

    def convolve(i, r):
        def product(kt):
            left = jnp.concatenate(
                [act[pl.ds(i * CHUNK + kt, CHUNK), 2 * r + kh].reshape(positions, 2 * chans) for kh in range(3)],
                axis=1,
            )
            return jnp.dot(left, w[kt].reshape(3 * 2 * chans, 2 * chans), preferred_element_type=jnp.float32)

        def kept(keep, value):
            mask = jnp.broadcast_to(keep[pl.ds(i * CHUNK, CHUNK)][:, None, :], (CHUNK, half, chans))
            mask = mask.reshape(positions, chans) > 0.5
            return jnp.concatenate(
                [jnp.where(mask, value[:, :chans], 0.0), jnp.where(mask, value[:, chans:], 0.0)], axis=1
            )

        both = product(2) + kept(keep1, product(1)) + kept(keep2, product(0))
        moved = jnp.where(inner == 0, 0.0, pltpu.roll(both[:, chans:], 1, axis=0))
        result = both[:, :chans] + moved + cbias_v[...]
        obuf[pl.ds(i * CHUNK, CHUNK), r] = result.astype(jnp.bfloat16).reshape(CHUNK, half, chans)

    def out_copy(i, r):
        return pltpu.make_async_copy(
            obuf.at[pl.ds(i * CHUNK, CHUNK), r], out.at[pl.ds(i * CHUNK, CHUNK), r], out_sem.at[r, i]
        )

    arrived(x.at[pl.ds(0, 2), pl.ds(1, rows)], recvh.at[1])
    for copy in weights:
        copy.wait()
    for frame in range(2):
        for row in range(1, rows + 1):
            activate(frame, row, frame * rows + row - 1)

    def lower(i, carry):
        for f in range(CHUNK):
            for row in range(1, rows + 1):
                activate(2 + i * CHUNK + f, row, f * rows + row - 1)
        convolve(i, 1)
        out_copy(i, 1).start()
        return carry

    lax.fori_loop(0, chunks, lower, 0)

    arrived(x.at[pl.ds(2, frames_n), 0], recvh.at[0])
    arrived(x.at[pl.ds(0, 2), 0], recvh.at[2])
    live = e > 0
    for frame in range(2):
        activate(frame, 0, frame, live)

    def upper(i, carry):
        for f in range(CHUNK):
            activate(2 + i * CHUNK + f, 0, f, live)
        convolve(i, 0)
        out_copy(i, 0).start()
        return carry

    lax.fori_loop(0, chunks, upper, 0)

    for copy in sent:
        copy.wait_send()
    for r in range(2):
        for i in range(chunks):
            out_copy(i, r).wait()


def local(frames, clip_of_frame, norm_gain, norm_bias, conv_weight, conv_bias):
    frames_n, rows, cols, chans = frames.shape
    half = cols // 2
    chunks = frames_n // CHUNK
    f32, bf16 = jnp.float32, jnp.bfloat16
    dma = pltpu.SemaphoreType.DMA
    return pl.pallas_call(
        kernel,
        out_shape=jax.ShapeDtypeStruct((frames_n, rows // 2, half, chans), bf16),
        in_specs=[pl.BlockSpec(memory_space=pl.ANY)] * 6,
        out_specs=pl.BlockSpec(memory_space=pl.ANY),
        scratch_shapes=[
            pltpu.VMEM((frames_n + 2, rows + 1, cols, chans), bf16),
            pltpu.VMEM((frames_n + 2, rows + 1, half, 2 * chans), bf16),
            pltpu.VMEM((CHUNK * rows, frames_n + CHUNK, chans), f32),
            pltpu.VMEM((3, 3, 2 * chans, 2 * chans), bf16),
            pltpu.VMEM((NK, CHUNK, chans), f32),
            pltpu.VMEM((NK, CHUNK, chans), f32),
            pltpu.VMEM((CHUNK, chans), f32),
            pltpu.VMEM((LOADERS * NX, CHUNK, chans), f32),
            pltpu.VMEM((LOADERS, CHUNK, chans), f32),
            pltpu.VMEM((LOADERS + 1, NK, CHUNK, chans), f32),
            pltpu.VMEM((frames_n + CHUNK, chans), f32),
            pltpu.VMEM((frames_n + CHUNK, chans), f32),
            pltpu.VMEM((frames_n, chans), f32),
            pltpu.VMEM((frames_n, chans), f32),
            pltpu.VMEM((frames_n, rows // 2, half, chans), bf16),
            pltpu.SMEM((2,), jnp.int32),
            pltpu.VMEM((1, chans), f32),
            pltpu.VMEM((1, chans), f32),
            pltpu.VMEM((1, chans), f32),
            dma((chunks,)),
            dma((4,)),
            dma((3,)),
            dma((2, chunks)),
            dma((32,)),
            dma((NK,)),
            dma((LOADERS * NX,)),
            dma((NK,)),
            dma((3,)),
        ],
        compiler_params=pltpu.CompilerParams(
            collective_id=0, has_side_effects=True, vmem_limit_bytes=48 * 1024 * 1024
        ),
    )(
        frames,
        clip_of_frame,
        norm_gain.reshape(1, chans),
        norm_bias.reshape(1, chans),
        conv_weight,
        conv_bias.reshape(1, chans),
    )


def solution(mesh):
    placed = (P("loader", "enc", None, None), P(("loader", "enc")), P(), P(), P(), P())
    return jax.shard_map(
        local, mesh=mesh, in_specs=placed, out_specs=P("loader", "enc", None, None), check_vma=False
    )
```

```python
import jax
import jax.numpy as jnp
from jax import lax
from jax.experimental import pallas as pl
from jax.experimental.pallas import tpu as pltpu
from jax.sharding import PartitionSpec as P

MESH = pl.DeviceIdType.MESH
EPS = 1e-06
GROUP = 4
LOADERS, NX, NZ, CORES = 4, 4, 4, 2
ENCS = NX * NZ * CORES
PIECE = 8
CHUNK = 8
EARLY, MIDDLE = 2, 8
BARRIER_AT = 4


def spread(values, lane, at):
    only = jnp.where(lane % GROUP == at, values, 0.0)
    width = values.shape[1]
    total = only
    for other in range(GROUP):
        if other != at:
            total = total + pltpu.roll(only, (other - at) % width, axis=1)
    return total


def kernel(
    frames, clips, gain, bias, weight, conv_bias, out,
    x, split, act, tmp, w, part, from_core, sum0, from_z, sum1, from_x, sum2, table,
    scale, shift, keep1, keep2, obuf, ids_s, gain_v, bias_v, cbias_v,
    load_sem, small_sem, w_sem, out_sem, send_sem, halo_send, recv_core, recv_z, recv_x, recv_y, recv_frames, recv_halo,
):
    frames_n, rows, cols, chans = frames.shape
    pieces, chunks = frames_n // PIECE, frames_n // CHUNK
    half = cols // 2
    l, e = lax.axis_index("loader"), lax.axis_index("enc")
    xi, z, c = e // (NZ * CORES), (e // CORES) % NZ, e % CORES

    def enc_at(xi, z, c):
        return (xi * NZ + z) * CORES + c

    l_next, l_prev = (l + 1) % LOADERS, (l + LOADERS - 1) % LOADERS
    e_next, e_prev = (e + 1) % ENCS, (e + ENCS - 1) % ENCS
    other_core = (l, enc_at(xi, z, 1 - c))
    along_z = [(l, enc_at(xi, (z + i) % NZ, c)) for i in range(1, NZ)]
    along_x = [(l, enc_at((xi + i) % NX, z, c)) for i in range(1, NX)]
    along_y = [((l + i) % LOADERS, e) for i in range(1, LOADERS)]

    barrier = pltpu.get_barrier_semaphore()
    senders = [other_core] + along_z + along_x + along_y + [(l, e_prev), (l_prev, e_prev)]
    for device in senders:
        pl.semaphore_signal(barrier, inc=1, device_id=device, device_id_type=MESH)

    loads = []
    for i in range(pieces):
        loads.append(
            pltpu.make_async_copy(
                frames.at[pl.ds(i * PIECE, PIECE)],
                x.at[pl.ds(2 + i * PIECE, PIECE), pl.ds(1, rows)],
                load_sem.at[i],
            )
        )
        loads[-1].start()
    smalls = [
        pltpu.make_async_copy(clips, ids_s, small_sem.at[0]),
        pltpu.make_async_copy(gain, gain_v, small_sem.at[1]),
        pltpu.make_async_copy(bias, bias_v, small_sem.at[2]),
        pltpu.make_async_copy(conv_bias, cbias_v, small_sem.at[3]),
    ]
    for copy in smalls:
        copy.start()
    weights = [
        pltpu.make_async_copy(weight.at[:, :, 1], w.at[:, :, pl.ds(0, chans), pl.ds(0, chans)], w_sem.at[0]),
        pltpu.make_async_copy(weight.at[:, :, 2], w.at[:, :, pl.ds(chans, chans), pl.ds(0, chans)], w_sem.at[1]),
        pltpu.make_async_copy(weight.at[:, :, 0], w.at[:, :, pl.ds(chans, chans), pl.ds(chans, chans)], w_sem.at[2]),
    ]
    for copy in weights:
        copy.start()

    def remote(src, dst, sent, recv, device):
        return pltpu.make_async_remote_copy(
            src_ref=src, dst_ref=dst, send_sem=sent, recv_sem=recv, device_id=device, device_id_type=MESH
        )

    def arrived(ref, sem):
        pltpu.make_async_copy(ref, ref, sem).wait()

    halos = [
        remote(
            frames.at[pl.ds(i * PIECE, PIECE), rows - 1],
            x.at[pl.ds(2 + i * PIECE, PIECE), 0],
            halo_send.at[i], recv_halo.at[i], (l, e_next),
        )
        for i in range(pieces)
    ]
    sent = [
        remote(frames.at[pl.ds(frames_n - 2, 2)], x.at[pl.ds(0, 2), pl.ds(1, rows)], send_sem.at[0], recv_frames.at[0], (l_next, e)),
        remote(frames.at[pl.ds(frames_n - 2, 2), rows - 1], x.at[pl.ds(0, 2), 0], send_sem.at[1], recv_frames.at[1], (l_next, e_next)),
    ]

    def start(copies):
        for copy in copies:
            copy.start()

    lane = lax.broadcasted_iota(jnp.int32, (PIECE, chans), 1)
    role = lane % GROUP
    sums = []
    for i in range(pieces):
        if i == BARRIER_AT:
            pl.semaphore_wait(barrier, len(senders))
            start(sent)
            start(halos[:EARLY])
        loads[i].wait()
        values = x[pl.ds(2 + i * PIECE, PIECE), pl.ds(1, rows)].astype(jnp.float32)
        first = jnp.sum(values, axis=(1, 2))
        second = jnp.sum(values * values, axis=(1, 2))
        for by in (1, 2):
            first = first + pltpu.roll(first, chans - by, axis=1)
            second = second + pltpu.roll(second, chans - by, axis=1)
        second = pltpu.roll(second, 1, axis=1)
        sums.append(jnp.where(role == 0, first, jnp.where(role == 1, second, 0.0)))
    smalls[0].wait()
    id_lane = (l % 2) * frames_n + 2 * e
    ids = jnp.where(
        lane == id_lane,
        (ids_s[0] + 1).astype(jnp.float32),
        jnp.where(lane == id_lane + 1, (ids_s[1] + 1).astype(jnp.float32), 0.0),
    )
    for core in range(CORES):
        for block in range(2):
            at = 4 * core + block
            part[core, pl.ds(block * PIECE, PIECE)] = sums[at] + pltpu.roll(sums[at + 2], 2, axis=1)
        part[core, pl.ds(2 * PIECE, PIECE)] = ids

    def exchange(value, slots, mine, sems, first_sem, devices):
        copies = [
            remote(value, slots.at[mine], send_sem.at[first_sem + i], sems.at[mine], device)
            for i, device in enumerate(devices)
        ]
        start(copies)
        return copies

    def collect(slots, mine, sems, count):
        for i in range(1, count):
            at = (mine + i) % count
            arrived(slots.at[at], sems.at[at])

    def divide(frame):
        for row in range(1, rows + 1):
            slot = row - 1
            tmp[slot] = x[frame, row].astype(jnp.float32)
            split[frame, row, :, pl.ds(0, chans)] = tmp[slot, pl.ds(0, half, stride=2)].astype(jnp.bfloat16)
            split[frame, row, :, pl.ds(chans, chans)] = tmp[slot, pl.ds(1, half, stride=2)].astype(jnp.bfloat16)

    def divide_some(first, last):
        def step(i, carry):
            for f in range(4):
                divide(2 + 4 * i + f)
            return carry

        lax.fori_loop(first, last, step, 0)

    to_core = remote(part.at[1 - c], from_core, send_sem.at[2], recv_core.at[0], other_core)
    to_core.start()
    sent.append(to_core)
    w[:, :, :chans, chans:] = jnp.zeros((3, 3, chans, chans), jnp.bfloat16)
    arrived(from_core, recv_core.at[0])
    sum0[...] = part[c] + from_core[...]
    sent += exchange(sum0, from_z, z, recv_z, 3, along_z)
    from_z[z] = sum0[...]
    steps = frames_n // 4
    divide_some(0, steps // 2)
    collect(from_z, z, recv_z, NZ)
    sum1[...] = jnp.sum(from_z[...], axis=0)
    sent += exchange(sum1, from_x, xi, recv_x, 6, along_x)
    from_x[xi] = sum1[...]
    start(halos[EARLY:MIDDLE])
    divide_some(steps // 2, steps)
    collect(from_x, xi, recv_x, NX)
    sum2[...] = jnp.sum(from_x[...], axis=0)
    sent += exchange(sum2, table.at[c], l, recv_y, 9, along_y)
    table[c, l] = sum2[...]
    start(halos[MIDDLE:])
    arrived(x.at[pl.ds(0, 2), pl.ds(1, rows)], recv_frames.at[0])
    for frame in range(2):
        divide(frame)
    collect(table.at[c], l, recv_y, LOADERS)
    to_core = remote(table.at[c], table.at[c], send_sem.at[12], recv_core.at[1], other_core)
    to_core.start()
    sent.append(to_core)
    for copy in smalls[1:] + weights:
        copy.wait()
    arrived(table.at[1 - c], recv_core.at[1])

    total, count = LOADERS * frames_n, frames_n + PIECE
    blocks = []
    for loader in range(LOADERS):
        for core in range(CORES):
            block = table[core, loader, pl.ds(0, 2 * PIECE)]
            blocks += [block, pltpu.roll(block, chans - 2, axis=1)]
    everything = jnp.concatenate(blocks, axis=0)
    lane_all = lax.broadcasted_iota(jnp.int32, (total, chans), 1) % GROUP
    everything = jnp.where(lane_all == 3, 1.0, everything)
    id_row = [table[0, loader, pl.ds(2 * PIECE, 1)] for loader in range(LOADERS)]
    id_row = jnp.concatenate([id_row[0] + id_row[1], id_row[2] + id_row[3]], axis=1)
    id_row = jnp.broadcast_to(id_row, (count, total))
    at_col = lax.broadcasted_iota(jnp.int32, (count, total), 1)
    at_row = lax.broadcasted_iota(jnp.int32, (count, total), 0) + (l * frames_n - PIECE)

    def id_before(by):
        return jnp.sum(jnp.where(at_col == at_row - by, id_row, 0.0), axis=1, keepdims=True)

    own = id_before(0)
    member = jnp.where((id_row == own) & (at_col <= at_row), 1.0, 0.0)
    run = jnp.dot(member, everything, precision=lax.Precision.HIGHEST, preferred_element_type=jnp.float32)
    lane_run = lax.broadcasted_iota(jnp.int32, (count, chans), 1)
    per = jnp.maximum(spread(run, lane_run, 3), 1.0) * float(ENCS * rows * cols * GROUP)
    mean = spread(run, lane_run, 0) / per
    var = spread(run, lane_run, 1) / per - mean * mean
    times = lax.rsqrt(var + EPS) * gain_v[...]
    scale[...] = 0.5 * times
    shift[...] = 0.5 * (bias_v[...] - mean * times)
    for keep, by in ((keep1, 1), (keep2, 2)):
        kept = jnp.where(id_before(by) == own, 1.0, 0.0)
        keep[...] = jnp.broadcast_to(kept[PIECE:], (frames_n, chans))

    def silu_of(value, frame):
        at = pl.ds(frame + PIECE - 2, 1)
        s, b = scale[at], shift[at]
        if value.shape[1] != chans:
            s, b = jnp.concatenate([s, s], axis=1), jnp.concatenate([b, b], axis=1)
        h = value.astype(jnp.float32) * s + b
        return h + h * jnp.tanh(h)

    def activate(frame):
        for row in range(1, rows + 1):
            act[frame, row] = silu_of(split[frame, row], frame).astype(jnp.bfloat16)

    def activate_halo(frame, slot):
        tmp[slot] = jnp.where(e > 0, silu_of(x[frame, 0], frame), 0.0)
        act[frame, 0, :, pl.ds(0, chans)] = tmp[slot, pl.ds(0, half, stride=2)].astype(jnp.bfloat16)
        act[frame, 0, :, pl.ds(chans, chans)] = tmp[slot, pl.ds(1, half, stride=2)].astype(jnp.bfloat16)

    positions = CHUNK * half
    inner = lax.broadcasted_iota(jnp.int32, (positions, chans), 0) % half

    def convolve(i, r):
        def product(kt):
            left = jnp.concatenate(
                [act[pl.ds(i * CHUNK + kt, CHUNK), 2 * r + kh].reshape(positions, 2 * chans) for kh in range(3)],
                axis=1,
            )
            return jnp.dot(left, w[kt].reshape(3 * 2 * chans, 2 * chans), preferred_element_type=jnp.float32)

        def kept(keep, value):
            mask = jnp.broadcast_to(keep[pl.ds(i * CHUNK, CHUNK)][:, None, :], (CHUNK, half, chans))
            mask = mask.reshape(positions, chans) > 0.5
            return jnp.concatenate(
                [jnp.where(mask, value[:, :chans], 0.0), jnp.where(mask, value[:, chans:], 0.0)], axis=1
            )

        both = product(2) + kept(keep1, product(1)) + kept(keep2, product(0))
        moved = jnp.where(inner == 0, 0.0, pltpu.roll(both[:, chans:], 1, axis=0))
        result = both[:, :chans] + moved + cbias_v[...]
        obuf[pl.ds(i * CHUNK, CHUNK), r] = result.astype(jnp.bfloat16).reshape(CHUNK, half, chans)

    def out_copy(i, r):
        return pltpu.make_async_copy(
            obuf.at[pl.ds(i * CHUNK, CHUNK), r], out.at[pl.ds(i * CHUNK, CHUNK), r], out_sem.at[r, i]
        )

    for frame in range(2):
        activate(frame)

    def lower(i, carry):
        for f in range(CHUNK):
            activate(2 + i * CHUNK + f)
        convolve(i, 1)
        out_copy(i, 1).start()
        return carry

    lax.fori_loop(0, chunks, lower, 0)

    arrived(x.at[pl.ds(0, 2), 0], recv_frames.at[1])
    for frame in range(2):
        activate_halo(frame, frame)

    def upper(i, carry):
        for j in range(CHUNK // PIECE):
            piece = i * (CHUNK // PIECE) + j
            arrived(x.at[pl.ds(2 + piece * PIECE, PIECE), 0], recv_halo.at[piece])
        for f in range(CHUNK):
            activate_halo(2 + i * CHUNK + f, f)
        convolve(i, 0)
        out_copy(i, 0).start()
        return carry

    lax.fori_loop(0, chunks, upper, 0)

    for copy in sent + halos:
        copy.wait_send()
    for r in range(2):
        for i in range(chunks):
            out_copy(i, r).wait()


def local(frames, clip_of_frame, norm_gain, norm_bias, conv_weight, conv_bias):
    frames_n, rows, cols, chans = frames.shape
    half = cols // 2
    pieces, chunks = frames_n // PIECE, frames_n // CHUNK
    f32, bf16 = jnp.float32, jnp.bfloat16
    dma = pltpu.SemaphoreType.DMA
    load = 3 * PIECE
    return pl.pallas_call(
        kernel,
        out_shape=jax.ShapeDtypeStruct((frames_n, rows // 2, half, chans), bf16),
        in_specs=[pl.BlockSpec(memory_space=pl.ANY)] * 6,
        out_specs=pl.BlockSpec(memory_space=pl.ANY),
        scratch_shapes=[
            pltpu.VMEM((frames_n + 2, rows + 1, cols, chans), bf16),
            pltpu.VMEM((frames_n + 2, rows + 1, half, 2 * chans), bf16),
            pltpu.VMEM((frames_n + 2, rows + 1, half, 2 * chans), bf16),
            pltpu.VMEM((CHUNK, cols, chans), f32),
            pltpu.VMEM((3, 3, 2 * chans, 2 * chans), bf16),
            pltpu.VMEM((CORES, load, chans), f32),
            pltpu.VMEM((load, chans), f32),
            pltpu.VMEM((load, chans), f32),
            pltpu.VMEM((NZ, load, chans), f32),
            pltpu.VMEM((load, chans), f32),
            pltpu.VMEM((NX, load, chans), f32),
            pltpu.VMEM((load, chans), f32),
            pltpu.VMEM((CORES, LOADERS, load, chans), f32),
            pltpu.VMEM((frames_n + PIECE, chans), f32),
            pltpu.VMEM((frames_n + PIECE, chans), f32),
            pltpu.VMEM((frames_n, chans), f32),
            pltpu.VMEM((frames_n, chans), f32),
            pltpu.VMEM((frames_n, rows // 2, half, chans), bf16),
            pltpu.SMEM((2,), jnp.int32),
            pltpu.VMEM((1, chans), f32),
            pltpu.VMEM((1, chans), f32),
            pltpu.VMEM((1, chans), f32),
            dma((pieces,)),
            dma((4,)),
            dma((3,)),
            dma((2, chunks)),
            dma((13,)),
            dma((pieces,)),
            dma((2,)),
            dma((NZ,)),
            dma((NX,)),
            dma((LOADERS,)),
            dma((2,)),
            dma((pieces,)),
        ],
        compiler_params=pltpu.CompilerParams(
            collective_id=0, has_side_effects=True, vmem_limit_bytes=60 * 1024 * 1024
        ),
    )(
        frames,
        clip_of_frame,
        norm_gain.reshape(1, chans),
        norm_bias.reshape(1, chans),
        conv_weight,
        conv_bias.reshape(1, chans),
    )


def solution(mesh):
    placed = (P("loader", "enc", None, None), P(("loader", "enc")), P(), P(), P(), P())
    return jax.shard_map(
        local, mesh=mesh, in_specs=placed, out_specs=P("loader", "enc", None, None), check_vma=False
    )
```

```python
import jax
import jax.numpy as jnp
from jax import lax
from jax.experimental import pallas as pl
from jax.experimental.pallas import tpu as pltpu
from jax.sharding import PartitionSpec as P

MESH = pl.DeviceIdType.MESH
EPS = 1e-06
GROUP = 4
LOADERS, NX, NZ, CORES = 4, 4, 4, 2
ENCS = NX * NZ * CORES
PIECE = 8
CHUNK = 8
EARLY, MIDDLE = 2, 8
BARRIER_AT = 4


def spread(values, lane, at):
    only = jnp.where(lane % GROUP == at, values, 0.0)
    width = values.shape[1]
    total = only
    for other in range(GROUP):
        if other != at:
            total = total + pltpu.roll(only, (other - at) % width, axis=1)
    return total


def kernel(
    frames, clips, gain, bias, weight, conv_bias, out,
    x, split, act, tmp, w, part, from_core, sum0, from_z, sum1, from_x, sum2, table,
    scale, shift, keep1, keep2, obuf, ids_s, gain_v, bias_v, cbias_v,
    load_sem, small_sem, w_sem, out_sem, send_sem, halo_send, recv_core, recv_z, recv_x, recv_y, recv_frames, recv_halo,
):
    frames_n, rows, cols, chans = frames.shape
    pieces, chunks = frames_n // PIECE, frames_n // CHUNK
    half = cols // 2
    l, e = lax.axis_index("loader"), lax.axis_index("enc")
    xi, z, c = e // (NZ * CORES), (e // CORES) % NZ, e % CORES

    def enc_at(xi, z, c):
        return (xi * NZ + z) * CORES + c

    l_next, l_prev = (l + 1) % LOADERS, (l + LOADERS - 1) % LOADERS
    e_next, e_prev = (e + 1) % ENCS, (e + ENCS - 1) % ENCS
    other_core = (l, enc_at(xi, z, 1 - c))
    along_z = [(l, enc_at(xi, (z + i) % NZ, c)) for i in range(1, NZ)]
    along_x = [(l, enc_at((xi + i) % NX, z, c)) for i in range(1, NX)]
    along_y = [((l + i) % LOADERS, e) for i in range(1, LOADERS)]

    barrier = pltpu.get_barrier_semaphore()
    senders = [other_core] + along_z + along_x + along_y + [(l, e_prev), (l_prev, e_prev)]
    for device in senders:
        pl.semaphore_signal(barrier, inc=1, device_id=device, device_id_type=MESH)

    loads = []
    for i in range(pieces):
        loads.append(
            pltpu.make_async_copy(
                frames.at[pl.ds(i * PIECE, PIECE)],
                x.at[pl.ds(2 + i * PIECE, PIECE), pl.ds(1, rows)],
                load_sem.at[i],
            )
        )
        loads[-1].start()
    smalls = [
        pltpu.make_async_copy(clips, ids_s, small_sem.at[0]),
        pltpu.make_async_copy(gain, gain_v, small_sem.at[1]),
        pltpu.make_async_copy(bias, bias_v, small_sem.at[2]),
        pltpu.make_async_copy(conv_bias, cbias_v, small_sem.at[3]),
    ]
    for copy in smalls:
        copy.start()
    weights = [
        pltpu.make_async_copy(weight.at[:, :, 1], w.at[:, :, pl.ds(0, chans), pl.ds(0, chans)], w_sem.at[0]),
        pltpu.make_async_copy(weight.at[:, :, 2], w.at[:, :, pl.ds(chans, chans), pl.ds(0, chans)], w_sem.at[1]),
        pltpu.make_async_copy(weight.at[:, :, 0], w.at[:, :, pl.ds(chans, chans), pl.ds(chans, chans)], w_sem.at[2]),
    ]
    for copy in weights:
        copy.start()

    def remote(src, dst, sent, recv, device):
        return pltpu.make_async_remote_copy(
            src_ref=src, dst_ref=dst, send_sem=sent, recv_sem=recv, device_id=device, device_id_type=MESH
        )

    def arrived(ref, sem):
        pltpu.make_async_copy(ref, ref, sem).wait()

    halos = [
        remote(
            frames.at[pl.ds(i * PIECE, PIECE), rows - 1],
            x.at[pl.ds(2 + i * PIECE, PIECE), 0],
            halo_send.at[i], recv_halo.at[i], (l, e_next),
        )
        for i in range(pieces)
    ]
    sent = [
        remote(frames.at[pl.ds(frames_n - 2, 2)], x.at[pl.ds(0, 2), pl.ds(1, rows)], send_sem.at[0], recv_frames.at[0], (l_next, e)),
        remote(frames.at[pl.ds(frames_n - 2, 2), rows - 1], x.at[pl.ds(0, 2), 0], send_sem.at[1], recv_frames.at[1], (l_next, e_next)),
    ]

    def start(copies):
        for copy in copies:
            copy.start()

    lane = lax.broadcasted_iota(jnp.int32, (PIECE, chans), 1)
    role = lane % GROUP
    sums = []
    for i in range(pieces):
        if i == BARRIER_AT:
            pl.semaphore_wait(barrier, len(senders))
            start(sent)
            start(halos[:EARLY])
        loads[i].wait()
        values = x[pl.ds(2 + i * PIECE, PIECE), pl.ds(1, rows)].astype(jnp.float32)
        first = jnp.sum(values, axis=(1, 2))
        second = jnp.sum(values * values, axis=(1, 2))
        for by in (1, 2):
            first = first + pltpu.roll(first, chans - by, axis=1)
            second = second + pltpu.roll(second, chans - by, axis=1)
        second = pltpu.roll(second, 1, axis=1)
        sums.append(jnp.where(role == 0, first, jnp.where(role == 1, second, 0.0)))
    smalls[0].wait()
    id_lane = (l % 2) * frames_n + 2 * e
    ids = jnp.where(
        lane == id_lane,
        (ids_s[0] + 1).astype(jnp.float32),
        jnp.where(lane == id_lane + 1, (ids_s[1] + 1).astype(jnp.float32), 0.0),
    )
    for core in range(CORES):
        for block in range(2):
            at = 4 * core + block
            part[core, pl.ds(block * PIECE, PIECE)] = sums[at] + pltpu.roll(sums[at + 2], 2, axis=1)
        part[core, pl.ds(2 * PIECE, PIECE)] = ids

    def exchange(value, slots, mine, sems, first_sem, devices):
        copies = [
            remote(value, slots.at[mine], send_sem.at[first_sem + i], sems.at[mine], device)
            for i, device in enumerate(devices)
        ]
        start(copies)
        return copies

    def collect(slots, mine, sems, count):
        for i in range(1, count):
            at = (mine + i) % count
            arrived(slots.at[at], sems.at[at])

    def divide(frame):
        for row in range(1, rows + 1):
            slot = row - 1
            tmp[slot] = x[frame, row].astype(jnp.float32)
            split[frame, row, :, pl.ds(0, chans)] = tmp[slot, pl.ds(0, half, stride=2)].astype(jnp.bfloat16)
            split[frame, row, :, pl.ds(chans, chans)] = tmp[slot, pl.ds(1, half, stride=2)].astype(jnp.bfloat16)

    def divide_some(first, last):
        def step(i, carry):
            for f in range(4):
                divide(2 + 4 * i + f)
            return carry

        lax.fori_loop(first, last, step, 0)

    to_core = remote(part.at[1 - c], from_core, send_sem.at[2], recv_core.at[0], other_core)
    to_core.start()
    sent.append(to_core)
    w[:, :, :chans, chans:] = jnp.zeros((3, 3, chans, chans), jnp.bfloat16)
    arrived(from_core, recv_core.at[0])
    sum0[...] = part[c] + from_core[...]
    sent += exchange(sum0, from_z, z, recv_z, 3, along_z)
    from_z[z] = sum0[...]
    steps = frames_n // 4
    divide_some(0, steps // 2)
    collect(from_z, z, recv_z, NZ)
    sum1[...] = jnp.sum(from_z[...], axis=0)
    sent += exchange(sum1, from_x, xi, recv_x, 6, along_x)
    from_x[xi] = sum1[...]
    start(halos[EARLY:MIDDLE])
    divide_some(steps // 2, steps)
    collect(from_x, xi, recv_x, NX)
    sum2[...] = jnp.sum(from_x[...], axis=0)
    sent += exchange(sum2, table.at[c], l, recv_y, 9, along_y)
    table[c, l] = sum2[...]
    start(halos[MIDDLE:])
    arrived(x.at[pl.ds(0, 2), pl.ds(1, rows)], recv_frames.at[0])
    for frame in range(2):
        divide(frame)
    collect(table.at[c], l, recv_y, LOADERS)
    to_core = remote(table.at[c], table.at[c], send_sem.at[12], recv_core.at[1], other_core)
    to_core.start()
    sent.append(to_core)
    for copy in smalls[1:] + weights:
        copy.wait()
    arrived(table.at[1 - c], recv_core.at[1])

    total, count = LOADERS * frames_n, frames_n + PIECE
    blocks = []
    for loader in range(LOADERS):
        for core in range(CORES):
            block = table[core, loader, pl.ds(0, 2 * PIECE)]
            blocks += [block, pltpu.roll(block, chans - 2, axis=1)]
    everything = jnp.concatenate(blocks, axis=0)
    lane_all = lax.broadcasted_iota(jnp.int32, (total, chans), 1) % GROUP
    everything = jnp.where(lane_all == 3, 1.0, everything)
    id_row = [table[0, loader, pl.ds(2 * PIECE, 1)] for loader in range(LOADERS)]
    id_row = jnp.concatenate([id_row[0] + id_row[1], id_row[2] + id_row[3]], axis=1)
    id_row = jnp.broadcast_to(id_row, (count, total))
    at_col = lax.broadcasted_iota(jnp.int32, (count, total), 1)
    at_row = lax.broadcasted_iota(jnp.int32, (count, total), 0) + (l * frames_n - PIECE)

    def id_before(by):
        return jnp.sum(jnp.where(at_col == at_row - by, id_row, 0.0), axis=1, keepdims=True)

    own = id_before(0)
    member = jnp.where((id_row == own) & (at_col <= at_row), 1.0, 0.0)
    run = jnp.dot(member, everything, precision=lax.Precision.HIGHEST, preferred_element_type=jnp.float32)
    lane_run = lax.broadcasted_iota(jnp.int32, (count, chans), 1)
    per = jnp.maximum(spread(run, lane_run, 3), 1.0) * float(ENCS * rows * cols * GROUP)
    mean = spread(run, lane_run, 0) / per
    var = spread(run, lane_run, 1) / per - mean * mean
    times = lax.rsqrt(var + EPS) * gain_v[...]
    scale[...] = 0.5 * times
    shift[...] = 0.5 * (bias_v[...] - mean * times)
    for keep, by in ((keep1, 1), (keep2, 2)):
        kept = jnp.where(id_before(by) == own, 1.0, 0.0)
        keep[...] = jnp.broadcast_to(kept[PIECE:], (frames_n, chans))

    def silu_of(value, frame):
        at = pl.ds(frame + PIECE - 2, 1)
        s, b = scale[at], shift[at]
        if value.shape[1] != chans:
            s, b = jnp.concatenate([s, s], axis=1), jnp.concatenate([b, b], axis=1)
        h = value.astype(jnp.float32) * s + b
        return h + h * jnp.tanh(h)

    def activate(frame):
        for row in range(1, rows + 1):
            act[frame, row] = silu_of(split[frame, row], frame).astype(jnp.bfloat16)

    def activate_halo(frame, slot):
        tmp[slot] = jnp.where(e > 0, silu_of(x[frame, 0], frame), 0.0)
        act[frame, 0, :, pl.ds(0, chans)] = tmp[slot, pl.ds(0, half, stride=2)].astype(jnp.bfloat16)
        act[frame, 0, :, pl.ds(chans, chans)] = tmp[slot, pl.ds(1, half, stride=2)].astype(jnp.bfloat16)

    positions = CHUNK * half
    inner = lax.broadcasted_iota(jnp.int32, (positions, chans), 0) % half

    def convolve(i, r):
        def product(kt):
            left = jnp.concatenate(
                [act[pl.ds(i * CHUNK + kt, CHUNK), 2 * r + kh].reshape(positions, 2 * chans) for kh in range(3)],
                axis=1,
            )
            return jnp.dot(left, w[kt].reshape(3 * 2 * chans, 2 * chans), preferred_element_type=jnp.float32)

        def kept(keep, value):
            mask = jnp.broadcast_to(keep[pl.ds(i * CHUNK, CHUNK)][:, None, :], (CHUNK, half, chans))
            mask = mask.reshape(positions, chans) > 0.5
            return jnp.concatenate(
                [jnp.where(mask, value[:, :chans], 0.0), jnp.where(mask, value[:, chans:], 0.0)], axis=1
            )

        both = product(2) + kept(keep1, product(1)) + kept(keep2, product(0))
        moved = jnp.where(inner == 0, 0.0, pltpu.roll(both[:, chans:], 1, axis=0))
        result = both[:, :chans] + moved + cbias_v[...]
        obuf[pl.ds(i * CHUNK, CHUNK), r] = result.astype(jnp.bfloat16).reshape(CHUNK, half, chans)

    def out_copy(r):
        return pltpu.make_async_copy(obuf.at[:, r], out.at[:, r], out_sem.at[r])

    def activate_chunk(i):
        for f in range(CHUNK):
            activate(2 + i * CHUNK + f)

    for frame in range(2):
        activate(frame)
    activate_chunk(0)
    for i in range(chunks):
        if i + 1 < chunks:
            activate_chunk(i + 1)
        convolve(i, 1)
    out_copy(1).start()

    for piece in range(pieces):
        arrived(x.at[pl.ds(2 + piece * PIECE, PIECE), 0], recv_halo.at[piece])
    arrived(x.at[pl.ds(0, 2), 0], recv_frames.at[1])

    def activate_halo_chunk(i):
        for f in range(CHUNK):
            activate_halo(2 + i * CHUNK + f, 2 + i * CHUNK + f)

    for frame in range(2):
        activate_halo(frame, frame)
    activate_halo_chunk(0)
    for i in range(chunks):
        if i + 1 < chunks:
            activate_halo_chunk(i + 1)
        convolve(i, 0)
    out_copy(0).start()

    for copy in sent + halos:
        copy.wait_send()
    for r in range(2):
        out_copy(r).wait()


def local(frames, clip_of_frame, norm_gain, norm_bias, conv_weight, conv_bias):
    frames_n, rows, cols, chans = frames.shape
    half = cols // 2
    pieces, chunks = frames_n // PIECE, frames_n // CHUNK
    f32, bf16 = jnp.float32, jnp.bfloat16
    dma = pltpu.SemaphoreType.DMA
    load = 3 * PIECE
    return pl.pallas_call(
        kernel,
        out_shape=jax.ShapeDtypeStruct((frames_n, rows // 2, half, chans), bf16),
        in_specs=[pl.BlockSpec(memory_space=pl.ANY)] * 6,
        out_specs=pl.BlockSpec(memory_space=pl.ANY),
        scratch_shapes=[
            pltpu.VMEM((frames_n + 2, rows + 1, cols, chans), bf16),
            pltpu.VMEM((frames_n + 2, rows + 1, half, 2 * chans), bf16),
            pltpu.VMEM((frames_n + 2, rows + 1, half, 2 * chans), bf16),
            pltpu.VMEM((frames_n + 2, cols, chans), f32),
            pltpu.VMEM((3, 3, 2 * chans, 2 * chans), bf16),
            pltpu.VMEM((CORES, load, chans), f32),
            pltpu.VMEM((load, chans), f32),
            pltpu.VMEM((load, chans), f32),
            pltpu.VMEM((NZ, load, chans), f32),
            pltpu.VMEM((load, chans), f32),
            pltpu.VMEM((NX, load, chans), f32),
            pltpu.VMEM((load, chans), f32),
            pltpu.VMEM((CORES, LOADERS, load, chans), f32),
            pltpu.VMEM((frames_n + PIECE, chans), f32),
            pltpu.VMEM((frames_n + PIECE, chans), f32),
            pltpu.VMEM((frames_n, chans), f32),
            pltpu.VMEM((frames_n, chans), f32),
            pltpu.VMEM((frames_n, rows // 2, half, chans), bf16),
            pltpu.SMEM((2,), jnp.int32),
            pltpu.VMEM((1, chans), f32),
            pltpu.VMEM((1, chans), f32),
            pltpu.VMEM((1, chans), f32),
            dma((pieces,)),
            dma((4,)),
            dma((3,)),
            dma((2,)),
            dma((13,)),
            dma((pieces,)),
            dma((2,)),
            dma((NZ,)),
            dma((NX,)),
            dma((LOADERS,)),
            dma((2,)),
            dma((pieces,)),
        ],
        compiler_params=pltpu.CompilerParams(
            collective_id=0, has_side_effects=True, vmem_limit_bytes=60 * 1024 * 1024
        ),
    )(
        frames,
        clip_of_frame,
        norm_gain.reshape(1, chans),
        norm_bias.reshape(1, chans),
        conv_weight,
        conv_bias.reshape(1, chans),
    )


def solution(mesh):
    placed = (P("loader", "enc", None, None), P(("loader", "enc")), P(), P(), P(), P())
    return jax.shard_map(
        local, mesh=mesh, in_specs=placed, out_specs=P("loader", "enc", None, None), check_vma=False
    )
```

```python
import jax
import jax.numpy as jnp
from jax import lax
from jax.experimental import pallas as pl
from jax.experimental.pallas import tpu as pltpu
from jax.sharding import PartitionSpec as P

MESH = pl.DeviceIdType.MESH
EPS = 1e-06
GROUP = 4
LOADERS, NX, NZ, CORES = 4, 4, 4, 2
ENCS = NX * NZ * CORES
PIECE = 8
CHUNK = 8
EARLY = 2
BARRIER_AT = 4


def spread(values, lane, at):
    only = jnp.where(lane % GROUP == at, values, 0.0)
    width = values.shape[1]
    total = only
    for other in range(GROUP):
        if other != at:
            total = total + pltpu.roll(only, (other - at) % width, axis=1)
    return total


def kernel(
    frames, clips, gain, bias, weight, conv_bias, out,
    x, split, act, tmp, w, part, from_chips, sum1, from_plane, table,
    scale, shift, keep1, keep2, ids_s, gain_v, bias_v, cbias_v,
    load_sem, small_sem, w_sem, send_sem, halo_send, recv_chips, recv_plane, recv_core, recv_frames, recv_halo,
):
    frames_n, rows, cols, chans = frames.shape
    pieces, chunks = frames_n // PIECE, frames_n // CHUNK
    half = cols // 2
    l, e = lax.axis_index("loader"), lax.axis_index("enc")
    xi, z, c = e // (NZ * CORES), (e // CORES) % NZ, e % CORES

    def enc_at(xi, z, c):
        return (xi * NZ + z) * CORES + c

    l_next, l_prev = (l + 1) % LOADERS, (l + LOADERS - 1) % LOADERS
    e_next, e_prev = (e + 1) % ENCS, (e + ENCS - 1) % ENCS
    other_core = (l, enc_at(xi, z, 1 - c))
    column = [(i, j) for i in range(NZ) for j in range(CORES) if (i, j) != (0, 0)]
    column_devices = [(l, enc_at(xi, (z + i) % NZ, (c + j) % CORES)) for i, j in column]
    plane = [(i, j) for i in range(LOADERS) for j in range(NX) if (i, j) != (0, 0)]
    plane_devices = [((l + i) % LOADERS, enc_at((xi + j) % NX, z, c)) for i, j in plane]

    barrier = pltpu.get_barrier_semaphore()
    senders = column_devices + plane_devices + [(l, e_prev), (l_prev, e_prev)]
    for device in senders:
        pl.semaphore_signal(barrier, inc=1, device_id=device, device_id_type=MESH)

    loads = []
    for i in range(pieces):
        loads.append(
            pltpu.make_async_copy(
                frames.at[pl.ds(i * PIECE, PIECE)],
                x.at[pl.ds(2 + i * PIECE, PIECE), pl.ds(1, rows)],
                load_sem.at[i],
            )
        )
        loads[-1].start()
    smalls = [
        pltpu.make_async_copy(clips, ids_s, small_sem.at[0]),
        pltpu.make_async_copy(gain, gain_v, small_sem.at[1]),
        pltpu.make_async_copy(bias, bias_v, small_sem.at[2]),
        pltpu.make_async_copy(conv_bias, cbias_v, small_sem.at[3]),
    ]
    for copy in smalls:
        copy.start()
    weights = [
        pltpu.make_async_copy(weight.at[:, :, 1], w.at[:, :, pl.ds(0, chans), pl.ds(0, chans)], w_sem.at[0]),
        pltpu.make_async_copy(weight.at[:, :, 2], w.at[:, :, pl.ds(chans, chans), pl.ds(0, chans)], w_sem.at[1]),
        pltpu.make_async_copy(weight.at[:, :, 0], w.at[:, :, pl.ds(chans, chans), pl.ds(chans, chans)], w_sem.at[2]),
    ]
    for copy in weights:
        copy.start()

    def remote(src, dst, sent, recv, device):
        return pltpu.make_async_remote_copy(
            src_ref=src, dst_ref=dst, send_sem=sent, recv_sem=recv, device_id=device, device_id_type=MESH
        )

    def arrived(ref, sem):
        pltpu.make_async_copy(ref, ref, sem).wait()

    halos = [
        remote(
            frames.at[pl.ds(i * PIECE, PIECE), rows - 1],
            x.at[pl.ds(2 + i * PIECE, PIECE), 0],
            halo_send.at[i], recv_halo.at[i], (l, e_next),
        )
        for i in range(pieces)
    ]
    sent = [
        remote(frames.at[pl.ds(frames_n - 2, 2)], x.at[pl.ds(0, 2), pl.ds(1, rows)], send_sem.at[0], recv_frames.at[0], (l_next, e)),
        remote(frames.at[pl.ds(frames_n - 2, 2), rows - 1], x.at[pl.ds(0, 2), 0], send_sem.at[1], recv_frames.at[1], (l_next, e_next)),
    ]

    def start(copies):
        for copy in copies:
            copy.start()

    lane = lax.broadcasted_iota(jnp.int32, (PIECE, chans), 1)
    role = lane % GROUP
    sums = []
    for i in range(pieces):
        if i == BARRIER_AT:
            pl.semaphore_wait(barrier, len(senders))
            start(sent)
            start(halos[:EARLY])
        loads[i].wait()
        values = x[pl.ds(2 + i * PIECE, PIECE), pl.ds(1, rows)].astype(jnp.float32)
        first = jnp.sum(values, axis=(1, 2))
        second = jnp.sum(values * values, axis=(1, 2))
        for by in (1, 2):
            first = first + pltpu.roll(first, chans - by, axis=1)
            second = second + pltpu.roll(second, chans - by, axis=1)
        second = pltpu.roll(second, 1, axis=1)
        sums.append(jnp.where(role == 0, first, jnp.where(role == 1, second, 0.0)))
    smalls[0].wait()
    id_lane = (l % 2) * frames_n + 2 * e
    ids = jnp.where(
        lane == id_lane,
        (ids_s[0] + 1).astype(jnp.float32),
        jnp.where(lane == id_lane + 1, (ids_s[1] + 1).astype(jnp.float32), 0.0),
    )
    for core in range(CORES):
        for block in range(2):
            at = 4 * core + block
            part[core, pl.ds(block * PIECE, PIECE)] = sums[at] + pltpu.roll(sums[at + 2], 2, axis=1)
        part[core, pl.ds(2 * PIECE, 1)] = ids[:1]

    def divide(frame):
        for row in range(1, rows + 1):
            slot = row - 1
            tmp[slot] = x[frame, row].astype(jnp.float32)
            split[frame, row, :, pl.ds(0, chans)] = tmp[slot, pl.ds(0, half, stride=2)].astype(jnp.bfloat16)
            split[frame, row, :, pl.ds(chans, chans)] = tmp[slot, pl.ds(1, half, stride=2)].astype(jnp.bfloat16)

    def divide_some(first, last):
        def step(i, carry):
            for f in range(4):
                divide(2 + 4 * i + f)
            return carry

        lax.fori_loop(first, last, step, 0)

    for n, ((i, j), device) in enumerate(zip(column, column_devices)):
        sent.append(remote(part.at[(c + j) % CORES], from_chips.at[z, c], send_sem.at[2 + n], recv_chips.at[z, c], device))
        sent[-1].start()
    w[:, :, :chans, chans:] = jnp.zeros((3, 3, chans, chans), jnp.bfloat16)
    from_chips[z, c] = part[c]
    steps = frames_n // 4
    divide_some(0, steps // 2)
    for i, j in column:
        at = ((z + i) % NZ, (c + j) % CORES)
        arrived(from_chips.at[at], recv_chips.at[at])
    sum1[...] = jnp.sum(from_chips[...], axis=(0, 1))
    for n, device in enumerate(plane_devices):
        sent.append(remote(sum1, from_plane.at[l, xi], send_sem.at[9 + n], recv_plane.at[l, xi], device))
        sent[-1].start()
    from_plane[l, xi] = sum1[...]
    start(halos[EARLY:])
    divide_some(steps // 2, steps)
    arrived(x.at[pl.ds(0, 2), pl.ds(1, rows)], recv_frames.at[0])
    for frame in range(2):
        divide(frame)
    for i, j in plane:
        at = ((l + i) % LOADERS, (xi + j) % NX)
        arrived(from_plane.at[at], recv_plane.at[at])
    for loader in range(LOADERS):
        table[c, loader] = jnp.sum(from_plane[loader], axis=0)
    to_core = remote(table.at[c], table.at[c], send_sem.at[24], recv_core.at[0], other_core)
    to_core.start()
    sent.append(to_core)
    for copy in smalls[1:] + weights:
        copy.wait()
    arrived(table.at[1 - c], recv_core.at[0])

    total, count = LOADERS * frames_n, frames_n + PIECE
    blocks = []
    for loader in range(LOADERS):
        for core in range(CORES):
            block = table[core, loader, pl.ds(0, 2 * PIECE)]
            blocks += [block, pltpu.roll(block, chans - 2, axis=1)]
    everything = jnp.concatenate(blocks, axis=0)
    lane_all = lax.broadcasted_iota(jnp.int32, (total, chans), 1) % GROUP
    everything = jnp.where(lane_all == 3, 1.0, everything)
    id_row = [table[0, loader, pl.ds(2 * PIECE, 1)] for loader in range(LOADERS)]
    id_row = jnp.concatenate([id_row[0] + id_row[1], id_row[2] + id_row[3]], axis=1)
    id_row = jnp.broadcast_to(id_row, (count, total))
    at_col = lax.broadcasted_iota(jnp.int32, (count, total), 1)
    at_row = lax.broadcasted_iota(jnp.int32, (count, total), 0) + (l * frames_n - PIECE)

    def id_before(by):
        return jnp.sum(jnp.where(at_col == at_row - by, id_row, 0.0), axis=1, keepdims=True)

    own = id_before(0)
    member = jnp.where((id_row == own) & (at_col <= at_row), 1.0, 0.0)
    run = jnp.dot(member, everything, precision=lax.Precision.HIGHEST, preferred_element_type=jnp.float32)
    lane_run = lax.broadcasted_iota(jnp.int32, (count, chans), 1)
    per = jnp.maximum(spread(run, lane_run, 3), 1.0) * float(ENCS * rows * cols * GROUP)
    mean = spread(run, lane_run, 0) / per
    var = spread(run, lane_run, 1) / per - mean * mean
    times = lax.rsqrt(var + EPS) * gain_v[...]
    scale[...] = 0.5 * times
    shift[...] = 0.5 * (bias_v[...] - mean * times)
    for keep, by in ((keep1, 1), (keep2, 2)):
        kept = jnp.where(id_before(by) == own, 1.0, 0.0)
        keep[...] = jnp.broadcast_to(kept[PIECE:], (frames_n, chans))

    def silu_of(value, frame):
        at = pl.ds(frame + PIECE - 2, 1)
        s, b = scale[at], shift[at]
        if value.shape[1] != chans:
            s, b = jnp.concatenate([s, s], axis=1), jnp.concatenate([b, b], axis=1)
        h = value.astype(jnp.float32) * s + b
        return h + h * jnp.tanh(h)

    def activate(frame):
        for row in range(1, rows + 1):
            act[frame, row] = silu_of(split[frame, row], frame).astype(jnp.bfloat16)

    def activate_halo(frame, slot):
        tmp[slot] = jnp.where(e > 0, silu_of(x[frame, 0], frame), 0.0)
        act[frame, 0, :, pl.ds(0, chans)] = tmp[slot, pl.ds(0, half, stride=2)].astype(jnp.bfloat16)
        act[frame, 0, :, pl.ds(chans, chans)] = tmp[slot, pl.ds(1, half, stride=2)].astype(jnp.bfloat16)

    positions = CHUNK * half
    inner = lax.broadcasted_iota(jnp.int32, (positions, chans), 0) % half

    def convolve(i, r):
        def product(kt):
            left = jnp.concatenate(
                [act[pl.ds(i * CHUNK + kt, CHUNK), 2 * r + kh].reshape(positions, 2 * chans) for kh in range(3)],
                axis=1,
            )
            return jnp.dot(left, w[kt].reshape(3 * 2 * chans, 2 * chans), preferred_element_type=jnp.float32)

        def kept(keep, value):
            mask = jnp.broadcast_to(keep[pl.ds(i * CHUNK, CHUNK)][:, None, :], (CHUNK, half, chans))
            mask = mask.reshape(positions, chans) > 0.5
            return jnp.concatenate(
                [jnp.where(mask, value[:, :chans], 0.0), jnp.where(mask, value[:, chans:], 0.0)], axis=1
            )

        both = product(2) + kept(keep1, product(1)) + kept(keep2, product(0))
        moved = jnp.where(inner == 0, 0.0, pltpu.roll(both[:, chans:], 1, axis=0))
        result = both[:, :chans] + moved + cbias_v[...]
        out[pl.ds(i * CHUNK, CHUNK), r] = result.astype(jnp.bfloat16).reshape(CHUNK, half, chans)

    def activate_chunk(i):
        for f in range(CHUNK):
            activate(2 + i * CHUNK + f)

    for frame in range(2):
        activate(frame)
    activate_chunk(0)
    for i in range(chunks):
        if i + 1 < chunks:
            activate_chunk(i + 1)
        convolve(i, 1)

    for piece in range(pieces):
        arrived(x.at[pl.ds(2 + piece * PIECE, PIECE), 0], recv_halo.at[piece])
    arrived(x.at[pl.ds(0, 2), 0], recv_frames.at[1])

    def activate_halo_chunk(i):
        for f in range(CHUNK):
            activate_halo(2 + i * CHUNK + f, 2 + i * CHUNK + f)

    for frame in range(2):
        activate_halo(frame, frame)
    activate_halo_chunk(0)
    for i in range(chunks):
        if i + 1 < chunks:
            activate_halo_chunk(i + 1)
        convolve(i, 0)

    for copy in sent + halos:
        copy.wait_send()


def local(frames, clip_of_frame, norm_gain, norm_bias, conv_weight, conv_bias):
    frames_n, rows, cols, chans = frames.shape
    half = cols // 2
    pieces, chunks = frames_n // PIECE, frames_n // CHUNK
    f32, bf16 = jnp.float32, jnp.bfloat16
    dma = pltpu.SemaphoreType.DMA
    load = 2 * PIECE + 1
    return pl.pallas_call(
        kernel,
        out_shape=pltpu.VMEM((frames_n, rows // 2, half, chans), bf16),
        in_specs=[pl.BlockSpec(memory_space=pl.ANY)] * 6,
        out_specs=pl.BlockSpec(memory_space=pltpu.VMEM),
        scratch_shapes=[
            pltpu.VMEM((frames_n + 2, rows + 1, cols, chans), bf16),
            pltpu.VMEM((frames_n + 2, rows + 1, half, 2 * chans), bf16),
            pltpu.VMEM((frames_n + 2, rows + 1, half, 2 * chans), bf16),
            pltpu.VMEM((frames_n + 2, cols, chans), f32),
            pltpu.VMEM((3, 3, 2 * chans, 2 * chans), bf16),
            pltpu.VMEM((CORES, load, chans), f32),
            pltpu.VMEM((NZ, CORES, load, chans), f32),
            pltpu.VMEM((load, chans), f32),
            pltpu.VMEM((LOADERS, NX, load, chans), f32),
            pltpu.VMEM((CORES, LOADERS, load, chans), f32),
            pltpu.VMEM((frames_n + PIECE, chans), f32),
            pltpu.VMEM((frames_n + PIECE, chans), f32),
            pltpu.VMEM((frames_n, chans), f32),
            pltpu.VMEM((frames_n, chans), f32),
            pltpu.SMEM((2,), jnp.int32),
            pltpu.VMEM((1, chans), f32),
            pltpu.VMEM((1, chans), f32),
            pltpu.VMEM((1, chans), f32),
            dma((pieces,)),
            dma((4,)),
            dma((3,)),
            dma((25,)),
            dma((pieces,)),
            dma((NZ, CORES)),
            dma((LOADERS, NX)),
            dma((1,)),
            dma((2,)),
            dma((pieces,)),
        ],
        compiler_params=pltpu.CompilerParams(
            collective_id=0, has_side_effects=True, vmem_limit_bytes=60 * 1024 * 1024
        ),
    )(
        frames,
        clip_of_frame,
        norm_gain.reshape(1, chans),
        norm_bias.reshape(1, chans),
        conv_weight,
        conv_bias.reshape(1, chans),
    )


def solution(mesh):
    placed = (P("loader", "enc", None, None), P(("loader", "enc")), P(), P(), P(), P())
    return jax.shard_map(
        local, mesh=mesh, in_specs=placed, out_specs=P("loader", "enc", None, None), check_vma=False
    )
```

```python
import jax
import jax.numpy as jnp
from jax import lax
from jax.experimental import pallas as pl
from jax.experimental.pallas import tpu as pltpu
from jax.sharding import PartitionSpec as P

MESH = pl.DeviceIdType.MESH
EPS = 1e-06
GROUP = 4
LOADERS, NX, NZ, CORES = 4, 4, 4, 2
ENCS = NX * NZ * CORES
PIECE = 8
CHUNK = 8
EARLY = 1
BARRIER_AT = 4
WAIT = 2


def spread(values, lane, at):
    only = jnp.where(lane % GROUP == at, values, 0.0)
    width = values.shape[1]
    total = only
    for other in range(GROUP):
        if other != at:
            total = total + pltpu.roll(only, (other - at) % width, axis=1)
    return total


def kernel(
    frames, clips, gain, bias, weight, conv_bias, out,
    x, split, act, tmp, w, part, from_chips, sum1, from_plane, table,
    scale, shift, keep1, keep2, ids_s, gain_v, bias_v, cbias_v,
    load_sem, small_sem, w_sem, send_sem, halo_send, recv_chips, recv_plane, recv_core, recv_frames, recv_halo,
):
    frames_n, rows, cols, chans = frames.shape
    pieces, chunks = frames_n // PIECE, frames_n // CHUNK
    half = cols // 2
    l, e = lax.axis_index("loader"), lax.axis_index("enc")
    xi, z, c = e // (NZ * CORES), (e // CORES) % NZ, e % CORES

    def enc_at(xi, z, c):
        return (xi * NZ + z) * CORES + c

    l_next, l_prev = (l + 1) % LOADERS, (l + LOADERS - 1) % LOADERS
    e_next, e_prev = (e + 1) % ENCS, (e + ENCS - 1) % ENCS
    other_core = (l, enc_at(xi, z, 1 - c))
    column = [(i, j) for i in range(NZ) for j in range(CORES) if (i, j) != (0, 0)]
    column_devices = [(l, enc_at(xi, (z + i) % NZ, (c + j) % CORES)) for i, j in column]
    plane = [(i, j) for i in range(LOADERS) for j in range(NX) if (i, j) != (0, 0)]
    plane_devices = [((l + i) % LOADERS, enc_at((xi + j) % NX, z, c)) for i, j in plane]

    loads = []
    for i in range(pieces):
        loads.append(
            pltpu.make_async_copy(
                frames.at[pl.ds(i * PIECE, PIECE)],
                x.at[pl.ds(2 + i * PIECE, PIECE), pl.ds(1, rows)],
                load_sem.at[i],
            )
        )
        loads[-1].start()
    smalls = [
        pltpu.make_async_copy(clips, ids_s, small_sem.at[0]),
        pltpu.make_async_copy(gain, gain_v, small_sem.at[1]),
        pltpu.make_async_copy(bias, bias_v, small_sem.at[2]),
        pltpu.make_async_copy(conv_bias, cbias_v, small_sem.at[3]),
    ]
    for copy in smalls:
        copy.start()
    barrier = pltpu.get_barrier_semaphore()
    senders = column_devices + plane_devices + [(l, e_prev), (l_prev, e_prev)]
    for device in senders:
        pl.semaphore_signal(barrier, inc=1, device_id=device, device_id_type=MESH)

    weights = [
        pltpu.make_async_copy(weight.at[:, :, 1], w.at[:, :, pl.ds(0, chans), pl.ds(0, chans)], w_sem.at[0]),
        pltpu.make_async_copy(weight.at[:, :, 2], w.at[:, :, pl.ds(chans, chans), pl.ds(0, chans)], w_sem.at[1]),
        pltpu.make_async_copy(weight.at[:, :, 0], w.at[:, :, pl.ds(chans, chans), pl.ds(chans, chans)], w_sem.at[2]),
    ]

    def remote(src, dst, sent, recv, device):
        return pltpu.make_async_remote_copy(
            src_ref=src, dst_ref=dst, send_sem=sent, recv_sem=recv, device_id=device, device_id_type=MESH
        )

    def arrived(ref, sem):
        pltpu.make_async_copy(ref, ref, sem).wait()

    halos = [
        remote(
            frames.at[pl.ds(i * PIECE, PIECE), rows - 1],
            x.at[pl.ds(2 + i * PIECE, PIECE), 0],
            halo_send.at[i], recv_halo.at[i], (l, e_next),
        )
        for i in range(pieces)
    ]
    sent = [
        remote(frames.at[pl.ds(frames_n - 2, 2)], x.at[pl.ds(0, 2), pl.ds(1, rows)], send_sem.at[0], recv_frames.at[0], (l_next, e)),
        remote(frames.at[pl.ds(frames_n - 2, 2), rows - 1], x.at[pl.ds(0, 2), 0], send_sem.at[1], recv_frames.at[1], (l_next, e_next)),
    ]

    def start(copies):
        for copy in copies:
            copy.start()

    lane = lax.broadcasted_iota(jnp.int32, (PIECE, chans), 1)
    role = lane % GROUP
    sums = []
    for i in range(pieces):
        if i == BARRIER_AT:
            pl.semaphore_wait(barrier, len(senders))
            start(sent)
            start(halos[:EARLY])
        loads[i].wait()
        first, second = [], []
        for f in range(PIECE):
            tiles = x[2 + i * PIECE + f, pl.ds(1, rows)].astype(jnp.float32).reshape(rows * cols // 8, 8, chans)
            one, two = [tiles[n] for n in range(4)], [tiles[n] * tiles[n] for n in range(4)]
            for n in range(4, rows * cols // 8):
                one[n % 4] = one[n % 4] + tiles[n]
                two[n % 4] = two[n % 4] + tiles[n] * tiles[n]
            first.append((one[0] + one[1]) + (one[2] + one[3]))
            second.append((two[0] + two[1]) + (two[2] + two[3]))
        first = jnp.sum(jnp.stack(first), axis=1)
        second = jnp.sum(jnp.stack(second), axis=1)
        sums.append(
            jnp.where(
                lane % 2 == 0, first + pltpu.roll(first, chans - 1, axis=1), second + pltpu.roll(second, 1, axis=1)
            )
        )
    smalls[0].wait()
    share = frames_n // CORES
    id_lane = l * share + (2 * e) % share
    ids = jnp.where(
        lane == id_lane,
        (ids_s[0] + 1).astype(jnp.float32),
        jnp.where(lane == id_lane + 1, (ids_s[1] + 1).astype(jnp.float32), 0.0),
    )[:1]
    for core in range(CORES):
        for block in range(2):
            at = 4 * core + block
            near, far = sums[at], sums[at + 2]
            part[core, pl.ds(block * PIECE, PIECE)] = jnp.where(
                role < 2, near + pltpu.roll(near, chans - 2, axis=1), far + pltpu.roll(far, 2, axis=1)
            )
        for owner in range(CORES):
            part[core, pl.ds(2 * PIECE + owner, 1)] = jnp.where(2 * e // share == owner, ids, 0.0)

    def divide(frame):
        for row in range(1, rows + 1):
            slot = row - 1
            tmp[slot] = x[frame, row].astype(jnp.float32)
            split[frame, row, :, pl.ds(0, chans)] = tmp[slot, pl.ds(0, half, stride=2)].astype(jnp.bfloat16)
            split[frame, row, :, pl.ds(chans, chans)] = tmp[slot, pl.ds(1, half, stride=2)].astype(jnp.bfloat16)

    def divide_some(first, last):
        def step(i, carry):
            for f in range(4):
                divide(2 + 4 * i + f)
            return carry

        lax.fori_loop(first, last, step, 0)

    for n, ((i, j), device) in enumerate(zip(column, column_devices)):
        sent.append(remote(part.at[(c + j) % CORES], from_chips.at[z, c], send_sem.at[2 + n], recv_chips.at[z, c], device))
        sent[-1].start()
    start(weights)
    w[:, :, :chans, chans:] = jnp.zeros((3, 3, chans, chans), jnp.bfloat16)
    from_chips[z, c] = part[c]
    steps = frames_n // 4
    divide_some(0, steps // 2)
    for i, j in column:
        at = ((z + i) % NZ, (c + j) % CORES)
        arrived(from_chips.at[at], recv_chips.at[at])
    sum1[...] = jnp.sum(from_chips[...], axis=(0, 1))
    for n, device in enumerate(plane_devices):
        sent.append(remote(sum1, from_plane.at[l, xi], send_sem.at[9 + n], recv_plane.at[l, xi], device))
        sent[-1].start()
    from_plane[l, xi] = sum1[...]
    start(halos[EARLY:])
    divide_some(steps // 2, steps)
    arrived(x.at[pl.ds(0, 2), pl.ds(1, rows)], recv_frames.at[0])
    for frame in range(2):
        divide(frame)
    for i, j in plane:
        at = ((l + i) % LOADERS, (xi + j) % NX)
        arrived(from_plane.at[at], recv_plane.at[at])
    for loader in range(LOADERS):
        table[c, loader] = jnp.sum(from_plane[loader], axis=0)
    to_core = remote(table.at[c], table.at[c], send_sem.at[24], recv_core.at[0], other_core)
    to_core.start()
    sent.append(to_core)
    count = frames_n + PIECE
    at_row = lax.broadcasted_iota(jnp.int32, (count, chans), 0) + (l * frames_n - PIECE)
    place = lax.broadcasted_iota(jnp.int32, (count, chans), 1)
    frame_of = [(place // share) * frames_n + core * share + place % share for core in range(CORES)]
    id_of = []
    for core in range(CORES):
        row = table[c, 0, pl.ds(2 * PIECE + core, 1)]
        for loader in range(1, LOADERS):
            row = row + table[c, loader, pl.ds(2 * PIECE + core, 1)]
        id_of.append(jnp.broadcast_to(row, (count, chans)))

    def id_before(by):
        found = sum(jnp.where(at == at_row - by, row, 0.0) for at, row in zip(frame_of, id_of))
        return jnp.sum(found, axis=1, keepdims=True)

    own = id_before(0)
    for keep, by in ((keep1, 1), (keep2, 2)):
        kept = jnp.where(id_before(by) == own, 1.0, 0.0)
        keep[...] = jnp.broadcast_to(kept[PIECE:], (frames_n, chans))
    members = [jnp.where((row == own) & (at <= at_row), 1.0, 0.0) for at, row in zip(frame_of, id_of)]

    def half_of_run(core):
        blocks = []
        for loader in range(LOADERS):
            block = table[core, loader, pl.ds(0, 2 * PIECE)]
            blocks += [block, pltpu.roll(block, chans - 2, axis=1)]
        sums_of = jnp.where(place[:1] % GROUP == 3, 1.0, jnp.concatenate(blocks, axis=0))
        member = jnp.where(core == 0, members[0], members[1])
        return jnp.dot(member, sums_of, precision=lax.Precision.HIGHEST, preferred_element_type=jnp.float32)

    run = half_of_run(c)
    for copy in smalls[1:] + weights:
        copy.wait()
    arrived(table.at[1 - c], recv_core.at[0])
    run = run + half_of_run(1 - c)
    lane_run = lax.broadcasted_iota(jnp.int32, (count, chans), 1)
    per = jnp.maximum(spread(run, lane_run, 3), 1.0) * float(ENCS * rows * cols * GROUP)
    mean = spread(run, lane_run, 0) / per
    var = spread(run, lane_run, 1) / per - mean * mean
    times = lax.rsqrt(var + EPS) * gain_v[...]
    scale[...] = 0.5 * times
    shift[...] = 0.5 * (bias_v[...] - mean * times)
    def silu_of(value, frame):
        at = pl.ds(frame + PIECE - 2, 1)
        s, b = scale[at], shift[at]
        if value.shape[1] != chans:
            s, b = jnp.concatenate([s, s], axis=1), jnp.concatenate([b, b], axis=1)
        h = value.astype(jnp.float32) * s + b
        return h + h * jnp.tanh(h)

    def activate(frame):
        for row in range(1, rows + 1):
            act[frame, row] = silu_of(split[frame, row], frame).astype(jnp.bfloat16)

    def activate_halo(frame, slot):
        tmp[slot] = jnp.where(e > 0, silu_of(x[frame, 0], frame), 0.0)
        act[frame, 0, :, pl.ds(0, chans)] = tmp[slot, pl.ds(0, half, stride=2)].astype(jnp.bfloat16)
        act[frame, 0, :, pl.ds(chans, chans)] = tmp[slot, pl.ds(1, half, stride=2)].astype(jnp.bfloat16)

    positions = CHUNK * half
    inner = lax.broadcasted_iota(jnp.int32, (positions, chans), 0) % half

    def convolve(i, r):
        def product(kt):
            left = jnp.concatenate(
                [act[pl.ds(i * CHUNK + kt, CHUNK), 2 * r + kh].reshape(positions, 2 * chans) for kh in range(3)],
                axis=1,
            )
            return jnp.dot(left, w[kt].reshape(3 * 2 * chans, 2 * chans), preferred_element_type=jnp.float32)

        def kept(keep, value):
            mask = jnp.broadcast_to(keep[pl.ds(i * CHUNK, CHUNK)][:, None, :], (CHUNK, half, chans))
            mask = mask.reshape(positions, chans) > 0.5
            return jnp.concatenate(
                [jnp.where(mask, value[:, :chans], 0.0), jnp.where(mask, value[:, chans:], 0.0)], axis=1
            )

        both = product(2) + kept(keep1, product(1)) + kept(keep2, product(0))
        moved = jnp.where(inner == 0, 0.0, pltpu.roll(both[:, chans:], 1, axis=0))
        result = both[:, :chans] + moved + cbias_v[...]
        out[pl.ds(i * CHUNK, CHUNK), r] = result.astype(jnp.bfloat16).reshape(CHUNK, half, chans)

    def activate_chunk(i):
        for f in range(CHUNK):
            activate(2 + i * CHUNK + f)

    for frame in range(2):
        activate(frame)
    activate_chunk(0)
    for i in range(chunks):
        if i + 1 < chunks:
            activate_chunk(i + 1)
        convolve(i, 1)

    def await_halo(first, last):
        for piece in range(first, last):
            arrived(x.at[pl.ds(2 + piece * PIECE, PIECE), 0], recv_halo.at[piece])

    arrived(x.at[pl.ds(0, 2), 0], recv_frames.at[1])

    def activate_halo_chunk(i):
        for f in range(CHUNK):
            activate_halo(2 + i * CHUNK + f, 2 + i * CHUNK + f)

    for frame in range(2):
        activate_halo(frame, frame)
    await_halo(0, WAIT)
    activate_halo_chunk(0)
    for i in range(chunks):
        if i + 1 < chunks:
            if (i + 1) % WAIT == 0:
                await_halo(i + 1, min(i + 1 + WAIT, pieces))
            activate_halo_chunk(i + 1)
        convolve(i, 0)

    for copy in sent + halos:
        copy.wait_send()


def local(frames, clip_of_frame, norm_gain, norm_bias, conv_weight, conv_bias):
    frames_n, rows, cols, chans = frames.shape
    half = cols // 2
    pieces, chunks = frames_n // PIECE, frames_n // CHUNK
    f32, bf16 = jnp.float32, jnp.bfloat16
    dma = pltpu.SemaphoreType.DMA
    load = 2 * PIECE + CORES
    return pl.pallas_call(
        kernel,
        out_shape=pltpu.VMEM((frames_n, rows // 2, half, chans), bf16),
        in_specs=[pl.BlockSpec(memory_space=pl.ANY)] * 6,
        out_specs=pl.BlockSpec(memory_space=pltpu.VMEM),
        scratch_shapes=[
            pltpu.VMEM((frames_n + 2, rows + 1, cols, chans), bf16),
            pltpu.VMEM((frames_n + 2, rows + 1, half, 2 * chans), bf16),
            pltpu.VMEM((frames_n + 2, rows + 1, half, 2 * chans), bf16),
            pltpu.VMEM((frames_n + 2, cols, chans), f32),
            pltpu.VMEM((3, 3, 2 * chans, 2 * chans), bf16),
            pltpu.VMEM((CORES, load, chans), f32),
            pltpu.VMEM((NZ, CORES, load, chans), f32),
            pltpu.VMEM((load, chans), f32),
            pltpu.VMEM((LOADERS, NX, load, chans), f32),
            pltpu.VMEM((CORES, LOADERS, load, chans), f32),
            pltpu.VMEM((frames_n + PIECE, chans), f32),
            pltpu.VMEM((frames_n + PIECE, chans), f32),
            pltpu.VMEM((frames_n, chans), f32),
            pltpu.VMEM((frames_n, chans), f32),
            pltpu.SMEM((2,), jnp.int32),
            pltpu.VMEM((1, chans), f32),
            pltpu.VMEM((1, chans), f32),
            pltpu.VMEM((1, chans), f32),
            dma((pieces,)),
            dma((4,)),
            dma((3,)),
            dma((25,)),
            dma((pieces,)),
            dma((NZ, CORES)),
            dma((LOADERS, NX)),
            dma((1,)),
            dma((2,)),
            dma((pieces,)),
        ],
        compiler_params=pltpu.CompilerParams(
            collective_id=0, has_side_effects=True, vmem_limit_bytes=60 * 1024 * 1024
        ),
    )(
        frames,
        clip_of_frame,
        norm_gain.reshape(1, chans),
        norm_bias.reshape(1, chans),
        conv_weight,
        conv_bias.reshape(1, chans),
    )


def solution(mesh):
    placed = (P("loader", "enc", None, None), P(("loader", "enc")), P(), P(), P(), P())
    return jax.shard_map(
        local, mesh=mesh, in_specs=placed, out_specs=P("loader", "enc", None, None), check_vma=False
    )
```

```python
import jax
import jax.numpy as jnp
from jax import lax
from jax.experimental import pallas as pl
from jax.experimental.pallas import tpu as pltpu
from jax.sharding import PartitionSpec as P

MESH = pl.DeviceIdType.MESH
EPS = 1e-06
GROUP = 4
LOADERS, NX, NZ, CORES = 4, 4, 4, 2
ENCS = NX * NZ * CORES
PIECE = 8
CHUNK = 8
EARLY = 1
BARRIER_AT = 4
WAIT = 2


def spread(values, lane, at):
    only = jnp.where(lane % GROUP == at, values, 0.0)
    width = values.shape[1]
    total = only
    for other in range(GROUP):
        if other != at:
            total = total + pltpu.roll(only, (other - at) % width, axis=1)
    return total


def kernel(
    frames, clips, gain, bias, weight, conv_bias, out,
    x, split, act, tmp, w, part, from_chips, sum1, from_plane, table,
    scale, shift, keep1, keep2, ids_s, gain_v, bias_v, cbias_v,
    load_sem, small_sem, w_sem, send_sem, halo_send, recv_chips, recv_plane, recv_core, recv_frames, recv_halo,
):
    frames_n, rows, cols, chans = frames.shape
    pieces, chunks = frames_n // PIECE, frames_n // CHUNK
    half = cols // 2
    l, e = lax.axis_index("loader"), lax.axis_index("enc")
    xi, z, c = e // (NZ * CORES), (e // CORES) % NZ, e % CORES

    def enc_at(xi, z, c):
        return (xi * NZ + z) * CORES + c

    l_next, l_prev = (l + 1) % LOADERS, (l + LOADERS - 1) % LOADERS
    e_next, e_prev = (e + 1) % ENCS, (e + ENCS - 1) % ENCS
    other_core = (l, enc_at(xi, z, 1 - c))
    column = [(i, j) for i in range(NZ) for j in range(CORES) if (i, j) != (0, 0)]
    column.sort(key=lambda at: (-min(at[0], NZ - at[0]), -at[1]))
    column_devices = [(l, enc_at(xi, (z + i) % NZ, (c + j) % CORES)) for i, j in column]
    plane = [(i, j) for i in range(LOADERS) for j in range(NX) if (i, j) != (0, 0)]
    plane.sort(key=lambda at: -min(at[0], LOADERS - at[0]) - min(at[1], NX - at[1]))
    plane_devices = [((l + i) % LOADERS, enc_at((xi + j) % NX, z, c)) for i, j in plane]

    loads = []
    for i in range(pieces):
        loads.append(
            pltpu.make_async_copy(
                frames.at[pl.ds(i * PIECE, PIECE)],
                x.at[pl.ds(2 + i * PIECE, PIECE), pl.ds(1, rows)],
                load_sem.at[i],
            )
        )
        loads[-1].start()
    smalls = [
        pltpu.make_async_copy(clips, ids_s, small_sem.at[0]),
        pltpu.make_async_copy(gain, gain_v, small_sem.at[1]),
        pltpu.make_async_copy(bias, bias_v, small_sem.at[2]),
        pltpu.make_async_copy(conv_bias, cbias_v, small_sem.at[3]),
    ]
    for copy in smalls:
        copy.start()
    barrier = pltpu.get_barrier_semaphore()
    senders = column_devices + plane_devices + [(l, e_prev), (l_prev, e_prev)]
    for device in senders:
        pl.semaphore_signal(barrier, inc=1, device_id=device, device_id_type=MESH)

    weights = [
        pltpu.make_async_copy(weight.at[:, :, 1], w.at[:, :, pl.ds(0, chans), pl.ds(0, chans)], w_sem.at[0]),
        pltpu.make_async_copy(weight.at[:, :, 2], w.at[:, :, pl.ds(chans, chans), pl.ds(0, chans)], w_sem.at[1]),
        pltpu.make_async_copy(weight.at[:, :, 0], w.at[:, :, pl.ds(chans, chans), pl.ds(chans, chans)], w_sem.at[2]),
    ]

    def remote(src, dst, sent, recv, device):
        return pltpu.make_async_remote_copy(
            src_ref=src, dst_ref=dst, send_sem=sent, recv_sem=recv, device_id=device, device_id_type=MESH
        )

    def arrived(ref, sem):
        pltpu.make_async_copy(ref, ref, sem).wait()

    halos = [
        remote(
            frames.at[pl.ds(i * PIECE, PIECE), rows - 1],
            x.at[pl.ds(2 + i * PIECE, PIECE), 0],
            halo_send.at[i], recv_halo.at[i], (l, e_next),
        )
        for i in range(pieces)
    ]
    sent = [
        remote(frames.at[pl.ds(frames_n - 2, 2)], x.at[pl.ds(0, 2), pl.ds(1, rows)], send_sem.at[0], recv_frames.at[0], (l_next, e)),
        remote(frames.at[pl.ds(frames_n - 2, 2), rows - 1], x.at[pl.ds(0, 2), 0], send_sem.at[1], recv_frames.at[1], (l_next, e_next)),
    ]

    def start(copies):
        for copy in copies:
            copy.start()

    lane = lax.broadcasted_iota(jnp.int32, (PIECE, chans), 1)
    role = lane % GROUP
    sums = []
    for i in range(pieces):
        if i == BARRIER_AT:
            pl.semaphore_wait(barrier, len(senders))
            start(sent)
            start(halos[:EARLY])
        loads[i].wait()
        first, second = [], []
        for f in range(PIECE):
            tiles = x[2 + i * PIECE + f, pl.ds(1, rows)].astype(jnp.float32).reshape(rows * cols // 8, 8, chans)
            one, two = [tiles[n] for n in range(4)], [tiles[n] * tiles[n] for n in range(4)]
            for n in range(4, rows * cols // 8):
                one[n % 4] = one[n % 4] + tiles[n]
                two[n % 4] = two[n % 4] + tiles[n] * tiles[n]
            first.append((one[0] + one[1]) + (one[2] + one[3]))
            second.append((two[0] + two[1]) + (two[2] + two[3]))
        first = jnp.sum(jnp.stack(first), axis=1)
        second = jnp.sum(jnp.stack(second), axis=1)
        sums.append(
            jnp.where(
                lane % 2 == 0, first + pltpu.roll(first, chans - 1, axis=1), second + pltpu.roll(second, 1, axis=1)
            )
        )
    smalls[0].wait()
    share = frames_n // CORES
    id_lane = l * share + (2 * e) % share
    ids = jnp.where(
        lane == id_lane,
        (ids_s[0] + 1).astype(jnp.float32),
        jnp.where(lane == id_lane + 1, (ids_s[1] + 1).astype(jnp.float32), 0.0),
    )[:1]
    for core in range(CORES):
        for block in range(2):
            at = 4 * core + block
            near, far = sums[at], sums[at + 2]
            part[core, pl.ds(block * PIECE, PIECE)] = jnp.where(
                role < 2, near + pltpu.roll(near, chans - 2, axis=1), far + pltpu.roll(far, 2, axis=1)
            )
        for owner in range(CORES):
            part[core, pl.ds(2 * PIECE + owner, 1)] = jnp.where(2 * e // share == owner, ids, 0.0)

    def divide(frame):
        for row in range(1, rows + 1):
            slot = row - 1
            tmp[slot] = x[frame, row].astype(jnp.float32)
            split[frame, row, :, pl.ds(0, chans)] = tmp[slot, pl.ds(0, half, stride=2)].astype(jnp.bfloat16)
            split[frame, row, :, pl.ds(chans, chans)] = tmp[slot, pl.ds(1, half, stride=2)].astype(jnp.bfloat16)

    def divide_some(first, last):
        def step(i, carry):
            for f in range(4):
                divide(2 + 4 * i + f)
            return carry

        lax.fori_loop(first, last, step, 0)

    for n, ((i, j), device) in enumerate(zip(column, column_devices)):
        sent.append(remote(part.at[(c + j) % CORES], from_chips.at[z, c], send_sem.at[2 + n], recv_chips.at[z, c], device))
        sent[-1].start()
    start(weights)
    w[:, :, :chans, chans:] = jnp.zeros((3, 3, chans, chans), jnp.bfloat16)
    from_chips[z, c] = part[c]
    steps = frames_n // 4
    divide_some(0, steps // 2)
    for i, j in column:
        at = ((z + i) % NZ, (c + j) % CORES)
        arrived(from_chips.at[at], recv_chips.at[at])
    sum1[...] = jnp.sum(from_chips[...], axis=(0, 1))
    for n, device in enumerate(plane_devices):
        sent.append(remote(sum1, from_plane.at[l, xi], send_sem.at[9 + n], recv_plane.at[l, xi], device))
        sent[-1].start()
    from_plane[l, xi] = sum1[...]
    start(halos[EARLY:])
    divide_some(steps // 2, steps)
    arrived(x.at[pl.ds(0, 2), pl.ds(1, rows)], recv_frames.at[0])
    for frame in range(2):
        divide(frame)
    for i, j in plane:
        at = ((l + i) % LOADERS, (xi + j) % NX)
        arrived(from_plane.at[at], recv_plane.at[at])
    for loader in range(LOADERS):
        table[c, loader] = jnp.sum(from_plane[loader], axis=0)
    to_core = remote(table.at[c], table.at[c], send_sem.at[24], recv_core.at[0], other_core)
    to_core.start()
    sent.append(to_core)
    count = frames_n + PIECE
    at_row = lax.broadcasted_iota(jnp.int32, (count, chans), 0) + (l * frames_n - PIECE)
    place = lax.broadcasted_iota(jnp.int32, (count, chans), 1)
    frame_of = [(place // share) * frames_n + core * share + place % share for core in range(CORES)]
    id_of = []
    for core in range(CORES):
        row = table[c, 0, pl.ds(2 * PIECE + core, 1)]
        for loader in range(1, LOADERS):
            row = row + table[c, loader, pl.ds(2 * PIECE + core, 1)]
        id_of.append(jnp.broadcast_to(row, (count, chans)))

    def id_before(by):
        found = sum(jnp.where(at == at_row - by, row, 0.0) for at, row in zip(frame_of, id_of))
        return jnp.sum(found, axis=1, keepdims=True)

    own = id_before(0)
    for keep, by in ((keep1, 1), (keep2, 2)):
        kept = jnp.where(id_before(by) == own, 1.0, 0.0)
        keep[...] = jnp.broadcast_to(kept[PIECE:], (frames_n, chans))
    members = [jnp.where((row == own) & (at <= at_row), 1.0, 0.0) for at, row in zip(frame_of, id_of)]

    def half_of_run(core):
        blocks = []
        for loader in range(LOADERS):
            block = table[core, loader, pl.ds(0, 2 * PIECE)]
            blocks += [block, pltpu.roll(block, chans - 2, axis=1)]
        sums_of = jnp.where(place[:1] % GROUP == 3, 1.0, jnp.concatenate(blocks, axis=0))
        member = jnp.where(core == 0, members[0], members[1])
        return jnp.dot(member, sums_of, precision=lax.Precision.HIGHEST, preferred_element_type=jnp.float32)

    run = half_of_run(c)
    for copy in smalls[1:] + weights:
        copy.wait()
    arrived(table.at[1 - c], recv_core.at[0])
    run = run + half_of_run(1 - c)
    lane_run = lax.broadcasted_iota(jnp.int32, (count, chans), 1)
    per = jnp.maximum(spread(run, lane_run, 3), 1.0) * float(ENCS * rows * cols * GROUP)
    mean = spread(run, lane_run, 0) / per
    var = spread(run, lane_run, 1) / per - mean * mean
    times = lax.rsqrt(var + EPS) * gain_v[...]
    scale[...] = 0.5 * times
    shift[...] = 0.5 * (bias_v[...] - mean * times)
    def silu_of(value, frame):
        at = pl.ds(frame + PIECE - 2, 1)
        s, b = scale[at], shift[at]
        if value.shape[1] != chans:
            s, b = jnp.concatenate([s, s], axis=1), jnp.concatenate([b, b], axis=1)
        h = value.astype(jnp.float32) * s + b
        return h + h * jnp.tanh(h)

    def activate(frame):
        for row in range(1, rows + 1):
            act[frame, row] = silu_of(split[frame, row], frame).astype(jnp.bfloat16)

    def activate_halo(frame, slot):
        tmp[slot] = jnp.where(e > 0, silu_of(x[frame, 0], frame), 0.0)
        act[frame, 0, :, pl.ds(0, chans)] = tmp[slot, pl.ds(0, half, stride=2)].astype(jnp.bfloat16)
        act[frame, 0, :, pl.ds(chans, chans)] = tmp[slot, pl.ds(1, half, stride=2)].astype(jnp.bfloat16)

    positions = CHUNK * half
    inner = lax.broadcasted_iota(jnp.int32, (positions, chans), 0) % half

    def convolve(i, r):
        def product(kt):
            left = jnp.concatenate(
                [act[pl.ds(i * CHUNK + kt, CHUNK), 2 * r + kh].reshape(positions, 2 * chans) for kh in range(3)],
                axis=1,
            )
            return jnp.dot(left, w[kt].reshape(3 * 2 * chans, 2 * chans), preferred_element_type=jnp.float32)

        def kept(keep, value):
            mask = jnp.broadcast_to(keep[pl.ds(i * CHUNK, CHUNK)][:, None, :], (CHUNK, half, chans))
            mask = mask.reshape(positions, chans) > 0.5
            return jnp.concatenate(
                [jnp.where(mask, value[:, :chans], 0.0), jnp.where(mask, value[:, chans:], 0.0)], axis=1
            )

        both = product(2) + kept(keep1, product(1)) + kept(keep2, product(0))
        moved = jnp.where(inner == 0, 0.0, pltpu.roll(both[:, chans:], 1, axis=0))
        result = both[:, :chans] + moved + cbias_v[...]
        out[pl.ds(i * CHUNK, CHUNK), r] = result.astype(jnp.bfloat16).reshape(CHUNK, half, chans)

    def activate_chunk(i):
        for f in range(CHUNK):
            activate(2 + i * CHUNK + f)

    for frame in range(2):
        activate(frame)
    activate_chunk(0)
    for i in range(chunks):
        if i + 1 < chunks:
            activate_chunk(i + 1)
        convolve(i, 1)

    def await_halo(first, last):
        for piece in range(first, last):
            arrived(x.at[pl.ds(2 + piece * PIECE, PIECE), 0], recv_halo.at[piece])

    arrived(x.at[pl.ds(0, 2), 0], recv_frames.at[1])

    def activate_halo_chunk(i):
        for f in range(CHUNK):
            activate_halo(2 + i * CHUNK + f, 2 + i * CHUNK + f)

    for frame in range(2):
        activate_halo(frame, frame)
    await_halo(0, WAIT)
    activate_halo_chunk(0)
    for i in range(chunks):
        if i + 1 < chunks:
            if (i + 1) % WAIT == 0:
                await_halo(i + 1, min(i + 1 + WAIT, pieces))
            activate_halo_chunk(i + 1)
        convolve(i, 0)

    for copy in sent + halos:
        copy.wait_send()


def local(frames, clip_of_frame, norm_gain, norm_bias, conv_weight, conv_bias):
    frames_n, rows, cols, chans = frames.shape
    half = cols // 2
    pieces, chunks = frames_n // PIECE, frames_n // CHUNK
    f32, bf16 = jnp.float32, jnp.bfloat16
    dma = pltpu.SemaphoreType.DMA
    load = 2 * PIECE + CORES
    return pl.pallas_call(
        kernel,
        out_shape=pltpu.VMEM((frames_n, rows // 2, half, chans), bf16),
        in_specs=[pl.BlockSpec(memory_space=pl.ANY)] * 6,
        out_specs=pl.BlockSpec(memory_space=pltpu.VMEM),
        scratch_shapes=[
            pltpu.VMEM((frames_n + 2, rows + 1, cols, chans), bf16),
            pltpu.VMEM((frames_n + 2, rows + 1, half, 2 * chans), bf16),
            pltpu.VMEM((frames_n + 2, rows + 1, half, 2 * chans), bf16),
            pltpu.VMEM((frames_n + 2, cols, chans), f32),
            pltpu.VMEM((3, 3, 2 * chans, 2 * chans), bf16),
            pltpu.VMEM((CORES, load, chans), f32),
            pltpu.VMEM((NZ, CORES, load, chans), f32),
            pltpu.VMEM((load, chans), f32),
            pltpu.VMEM((LOADERS, NX, load, chans), f32),
            pltpu.VMEM((CORES, LOADERS, load, chans), f32),
            pltpu.VMEM((frames_n + PIECE, chans), f32),
            pltpu.VMEM((frames_n + PIECE, chans), f32),
            pltpu.VMEM((frames_n, chans), f32),
            pltpu.VMEM((frames_n, chans), f32),
            pltpu.SMEM((2,), jnp.int32),
            pltpu.VMEM((1, chans), f32),
            pltpu.VMEM((1, chans), f32),
            pltpu.VMEM((1, chans), f32),
            dma((pieces,)),
            dma((4,)),
            dma((3,)),
            dma((25,)),
            dma((pieces,)),
            dma((NZ, CORES)),
            dma((LOADERS, NX)),
            dma((1,)),
            dma((2,)),
            dma((pieces,)),
        ],
        compiler_params=pltpu.CompilerParams(
            collective_id=0, has_side_effects=True, vmem_limit_bytes=60 * 1024 * 1024
        ),
    )(
        frames,
        clip_of_frame,
        norm_gain.reshape(1, chans),
        norm_bias.reshape(1, chans),
        conv_weight,
        conv_bias.reshape(1, chans),
    )


def solution(mesh):
    placed = (P("loader", "enc", None, None), P(("loader", "enc")), P(), P(), P(), P())
    return jax.shard_map(
        local, mesh=mesh, in_specs=placed, out_specs=P("loader", "enc", None, None), check_vma=False
    )
```
